256 devices in a mesh: dap: 64 (over z, y, core), grp: 4 (over x).
Axes of the slice: x: 4, y: 4, z: 8, core: 2. Of those that a mesh axis runs over, the one named last changes fastest.
Arguments:
- homolog_stack: bfloat16 [256, 768, 256], P(None, 'dap'), may hold values from -6 to 6
- couple_embedding: bfloat16 [768, 768, 128], P('dap', 'grp'), may hold values from -3 to 3
- dyad_entry_matrix: bfloat16 [256, 64], replicated, may hold values from -0.375 to 0.375
- dyad_final_matrix: bfloat16 [1024, 128], replicated, may hold values from -0.75 to 0.75
- query_key_gate_matrix: bfloat16 [128, 512], replicated, may hold values from -0.5 to 0.5
- couple_offset_matrix: float32 [128, 4], replicated, may hold values from -24 to 24
- softmax_final_matrix: bfloat16 [128, 128], replicated, may hold values from -2 to 2
- strand_couple_filter: int32 [6, 6], replicated, may hold values from 0 to 1, as said below
Outputs:
- pair_mid: bfloat16 [768, 768, 128], P('dap', 'grp')
- tri_update: bfloat16 [768, 768, 128], P('dap', 'grp')
The draws below stay inside these ranges and needn't reach their ends.
Inputs may be any that keep to these rules, and one draw needn't show every extreme that they name: `strand_couple_filter`: Symmetric, with every diagonal tile 1.
All inputs are finite; a program needn't handle non-finite values.
Results may differ from the reference program's by a relative error of at most 0.025.
Values may be sent and summed in bfloat16 or wider, within the bound.
No kernel may reach another device: no remote copies, remote signals or barrier semaphores. Data moves between devices by JAX's collectives and lax.ppermute only.
A program may use at most 128 MiB of HBM per device.

```python
import math
import jax
import jax.numpy as jnp
from jax import lax

STACK_FEATURES = 256
CZ = 128
PRODUCT_FEATURES = 32
HEADS = 4
HEAD_DIM = 32
AMINO_TOTAL = 768
HOMOLOG_TOTAL = 256
TILE = 128
NT = 6
HC = 128


def draw_couple_offset_matrix(key, part):
    key = jax.random.fold_in(key, 7)
    first_key, second_key = jax.random.split(key)
    base_draw = jax.random.normal(first_key, (CZ, HEADS), jnp.float32)
    factor = jnp.exp(jax.random.uniform(second_key, (HEADS,), jnp.float32, math.log(3.0), math.log(12.0)))
    return jnp.clip(base_draw * factor[None, :] * CZ ** (-0.5), -24.0, 24.0)


def draw_strand_couple_filter(key, part):
    key = jax.random.fold_in(key, 3)
    first_key, second_key = jax.random.split(key)
    levels = jax.random.randint(first_key, (NT,), 1, 5)
    pair_draw = jax.random.randint(second_key, (NT, NT), 0, 4)
    upper_half = jnp.arange(NT)[:, None] <= jnp.arange(NT)[None, :]
    mirrored = jnp.where(upper_half, pair_draw, pair_draw.T)
    reach_level = jnp.minimum(levels[:, None], levels[None, :])
    diagonal = jnp.arange(NT)[:, None] == jnp.arange(NT)[None, :]
    return jnp.where((mirrored < reach_level) | diagonal, 1, 0).astype(jnp.int32)


def block_levels(key, dims, cuts, low, top_value):
    loudness = 1.0
    for position, blocks in cuts:
        heights = jax.random.uniform(jax.random.fold_in(jax.random.fold_in(key, 6), position), (blocks,), jnp.float32, low / len(cuts), top_value / len(cuts))
        loudness = loudness * jnp.repeat(jnp.exp(heights), dims[position] // blocks).reshape((-1,) + (1,) * (len(dims) - 1 - position))
    return loudness


def normal_values(own_key, extent, width, most, cuts=(), held_as=jnp.bfloat16):
    level = block_levels(own_key, extent, cuts, -0.22, 0.18) if cuts else 1.0
    drawn = jax.random.normal(own_key, extent, jnp.float32) * width * level
    return jnp.minimum(jnp.maximum(drawn, -most), most).astype(held_as)


def setup_inputs(seed: int = 0) -> dict:
    seeds = jax.random.split(jax.random.key(seed), 9)
    homolog_stack = normal_values(seeds[0], (HOMOLOG_TOTAL, AMINO_TOTAL, STACK_FEATURES), 1.0, 6.0, ((1, 64),))
    couple_embedding = normal_values(seeds[1], (AMINO_TOTAL, AMINO_TOTAL, CZ), 0.5, 3.0, ((0, 64), (1, 4)))
    dyad_entry_matrix = normal_values(seeds[2], (STACK_FEATURES, 2 * PRODUCT_FEATURES), STACK_FEATURES ** -0.5, 0.375)
    dyad_final_matrix = normal_values(seeds[3], (PRODUCT_FEATURES * PRODUCT_FEATURES, CZ), (PRODUCT_FEATURES * PRODUCT_FEATURES // 16) ** -0.5, 0.75)
    query_key_gate_matrix = normal_values(seeds[4], (CZ, 4 * HC), CZ ** -0.5, 0.5)
    couple_offset_matrix = draw_couple_offset_matrix(jax.random.fold_in(seeds[8], 71), 0)
    softmax_final_matrix = normal_values(seeds[6], (HC, CZ), (HC // 16) ** -0.5, 2.0)
    strand_couple_filter = draw_strand_couple_filter(jax.random.fold_in(seeds[8], 71), 0)
    return {"homolog_stack": homolog_stack, "couple_embedding": couple_embedding, "dyad_entry_matrix": dyad_entry_matrix, "dyad_final_matrix": dyad_final_matrix, "query_key_gate_matrix": query_key_gate_matrix, "couple_offset_matrix": couple_offset_matrix, "softmax_final_matrix": softmax_final_matrix, "strand_couple_filter": strand_couple_filter}


def standardise_features(values):
    widened = values.astype(jnp.float32)
    centered = widened - lax.optimization_barrier(jnp.mean(widened, axis=-1, keepdims=True))
    spread = lax.optimization_barrier(jnp.mean(centered * centered, axis=-1, keepdims=True))
    return centered * lax.rsqrt(spread + 1e-05)

def reference(homolog_stack, couple_embedding, dyad_entry_matrix, dyad_final_matrix, query_key_gate_matrix, couple_offset_matrix, softmax_final_matrix, strand_couple_filter):
    homolog_standardised = standardise_features(homolog_stack).astype(jnp.bfloat16)
    projected_values = jnp.dot(homolog_standardised, dyad_entry_matrix, preferred_element_type=jnp.float32).astype(jnp.bfloat16)
    left_proj = projected_values[:, :, :PRODUCT_FEATURES].astype(jnp.float32)
    right_proj = projected_values[:, :, PRODUCT_FEATURES:].astype(jnp.float32)

    def outer_row(row_item):
        left_row, pair_row = row_item
        outer_prod = jnp.einsum('sx,sjy->jxy', left_row, right_proj) * (1.0 / HOMOLOG_TOTAL)
        outer_prod = outer_prod.reshape(AMINO_TOTAL, PRODUCT_FEATURES * PRODUCT_FEATURES).astype(jnp.bfloat16)
        update = jnp.dot(outer_prod, dyad_final_matrix, preferred_element_type=jnp.float32)
        return (pair_row.astype(jnp.float32) + update).astype(jnp.bfloat16)
    pair_mid = lax.map(outer_row, (jnp.swapaxes(left_proj, 0, 1), couple_embedding))
    pair_norm = standardise_features(pair_mid).astype(jnp.bfloat16)
    tri_bias = jnp.einsum('jkz,zh->hjk', pair_norm.astype(jnp.float32), couple_offset_matrix, precision=lax.Precision.HIGHEST)
    tile_ids = (jnp.arange(AMINO_TOTAL) // TILE).astype(jnp.int32)
    keep_mask = strand_couple_filter[tile_ids][:, tile_ids].astype(jnp.float32)
    penalty = (keep_mask - 1.0) * 1000000000.0
    inner_width = HEADS * HEAD_DIM

    def attend_row(row_item):
        norm_row, penalty_row = row_item
        projected_row = jnp.dot(norm_row, query_key_gate_matrix, preferred_element_type=jnp.float32)
        queries = (projected_row[:, :inner_width] * HEAD_DIM ** (-0.5)).astype(jnp.bfloat16)
        key_value = projected_row[:, inner_width:3 * inner_width].astype(jnp.bfloat16)
        gate_values = jax.nn.sigmoid(projected_row[:, 3 * inner_width:])
        query_heads = queries.astype(jnp.float32).reshape(AMINO_TOTAL, HEADS, HEAD_DIM)
        key_heads = key_value[:, :inner_width].astype(jnp.float32).reshape(AMINO_TOTAL, HEADS, HEAD_DIM)
        value_heads = key_value[:, inner_width:].astype(jnp.float32).reshape(AMINO_TOTAL, HEADS, HEAD_DIM)
        logits = jnp.einsum('jhd,khd->hjk', query_heads, key_heads)
        logits = logits + tri_bias + penalty_row[None, None, :]
        top_score = lax.optimization_barrier(jnp.max(logits, axis=-1, keepdims=True))
        expo = jnp.exp(logits - top_score)
        weights = (expo / lax.optimization_barrier(jnp.sum(expo, axis=-1, keepdims=True))).astype(jnp.bfloat16)
        attended = jnp.einsum('hjk,khd->jhd', weights.astype(jnp.float32), value_heads)
        gated = (gate_values * attended.reshape(AMINO_TOTAL, inner_width)).astype(jnp.bfloat16)
        return jnp.dot(gated, softmax_final_matrix, preferred_element_type=jnp.float32).astype(jnp.bfloat16)
    tri_update = lax.map(attend_row, (pair_norm, penalty))
    return (pair_mid, tri_update)
```

```python
import jax
import jax.numpy as jnp
from jax import lax
from jax.experimental import pallas as pl
from jax.experimental.pallas import tpu as pltpu
from jax.sharding import PartitionSpec as P

BF = jnp.bfloat16
F32 = jnp.float32
NT = (((1,), (1,)), ((), ()))
NN = (((1,), (0,)), ((), ()))

ROWS, COLS, CH, HEADS, HD = 12, 192, 128, 4, 32
MSA, PF = 256, 32
BLK = ROWS * PF
LANES = 128
HALF = COLS - LANES
PAYLOAD = HEADS * ROWS + HEADS * ROWS // 2


def ring(n, k):
    return [(i, (i + k) % n) for i in range(n)]


def dot(a, b, dims):
    return lax.dot_general(a, b, dims, preferred_element_type=F32)


def opm_kernel(pos_ref, lt_ref, *refs):
    pieces = refs[: len(PIECES)]
    (wblk_ref, emb_ref, off_ref, mid_ref, norm_ref, bias_ref) = refs[len(PIECES) : len(PIECES) + 6]
    (right, outer, lhs, sems) = refs[len(PIECES) + 6 :]
    zl, y, c = pos_ref[0], pos_ref[1], pos_ref[2]
    copies = []
    for n, (dz, dy, dc, lo, rows) in enumerate(PIECES):
        src_z = lax.rem(zl + dz, 2)
        src_y = lax.rem(y + 4 - dy, 4)
        src_c = lax.rem(c + dc, 2)
        start = (src_z * 8 + src_y * 2 + src_c) * BLK + lo
        cp = pltpu.make_async_copy(
            pieces[n], right.at[pl.ds(pl.multiple_of(start, 64), rows)], sems.at[n]
        )
        cp.start()
        copies.append(cp)
    for cp in copies:
        cp.wait()
    chunk = 48
    for t in range(COLS // chunk):
        buf = t % 2
        res = dot(right[t * chunk * PF : (t + 1) * chunk * PF, :], lt_ref[...], NT)
        for q in range(3):
            outer[buf, q] = res[:, q * LANES : (q + 1) * LANES]
            for ch in range(PF):
                part = outer[buf, q, pl.ds(ch, chunk, stride=PF), :]
                lhs[
                    q * COLS + t * chunk : q * COLS + (t + 1) * chunk, ch * LANES : (ch + 1) * LANES
                ] = (part * (1.0 / MSA)).astype(BF)
    w = off_ref[...]
    w_hi = w.astype(BF)
    rest = w - w_hi.astype(F32)
    w_mid = rest.astype(BF)
    w_lo = (rest - w_mid.astype(F32)).astype(BF)
    w3 = jnp.concatenate([w_hi, w_mid, w_lo], axis=0)
    for q in range(3):
        acc = dot(lhs[q * COLS : (q + 1) * COLS, :], wblk_ref[...], NN)
        for r in range(4):
            i = 4 * q + r
            mid = (emb_ref[i].astype(F32) + acc[:, r * CH : (r + 1) * CH]).astype(BF)
            mid_ref[i] = mid
            wide = mid.astype(F32)
            cen = wide - jnp.mean(wide, axis=-1, keepdims=True)
            var = jnp.mean(cen * cen, axis=-1, keepdims=True)
            nrm = (cen * lax.rsqrt(var + 1e-05)).astype(BF)
            norm_ref[i] = nrm
            parts = dot(w3, nrm, NT)
            b = parts[0:4] + parts[8:12] + parts[16:20]
            for h in range(HEADS):
                bias_ref[h * ROWS + i : h * ROWS + i + 1, :] = b[h : h + 1, :LANES]
                row = HEADS * ROWS + (h % 2) * ROWS + i
                lane = (h // 2) * HALF
                bias_ref[row : row + 1, lane : lane + HALF] = b[h : h + 1, LANES:]


BASE_PIECES = [
    (0, 0, 0, BLK), (1, 0, 0, BLK), (0, 1, 0, BLK), (0, 3, 0, BLK), (1, 1, 0, BLK), (1, 3, 0, BLK),
    (0, 2, 0, BLK // 2), (0, 2, BLK // 2, BLK // 2), (1, 2, 0, BLK // 2), (1, 2, BLK // 2, BLK // 2),
]
PIECES = [(z, y, c, lo, rows) for c in range(2) for (z, y, lo, rows) in BASE_PIECES]


def opm(pos, left, pieces, wblk, emb, off):
    vmem = pl.BlockSpec(memory_space=pltpu.VMEM)
    return pl.pallas_call(
        opm_kernel,
        out_shape=(
            jax.ShapeDtypeStruct((ROWS, COLS, CH), BF),
            jax.ShapeDtypeStruct((ROWS, COLS, CH), BF),
            jax.ShapeDtypeStruct((PAYLOAD, LANES), F32),
        ),
        in_specs=[pl.BlockSpec(memory_space=pltpu.SMEM), vmem]
        + [pl.BlockSpec(memory_space=pl.ANY)] * len(PIECES)
        + [vmem] * 3,
        out_specs=[vmem] * 3,
        scratch_shapes=[
            pltpu.VMEM((16 * BLK, MSA), BF),
            pltpu.VMEM((2, 3, 48 * PF, LANES), F32),
            pltpu.VMEM((3 * COLS, PF * LANES), BF),
            pltpu.SemaphoreType.DMA((len(PIECES),)),
        ],
        compiler_params=pltpu.CompilerParams(vmem_limit_bytes=56 * 1024 * 1024),
        cost_estimate=pl.CostEstimate(flops=6 * 10**9, bytes_accessed=10**7, transcendentals=0),
        name="opm",
    )(pos, left, *pieces, wblk, emb, off)


def attend_kernel(
    pos_ref, own_ref, prev_ref, next_ref, far_a_ref, far_b_ref, pay0_ref, pay1_ref, pen_ref,
    wqg_ref, wkv_ref, wo_ref, out_ref, bias,
):
    i = pl.program_id(0)
    z, y, c, x = pos_ref[0], pos_ref[1], pos_ref[2], pos_ref[3]

    @pl.when(i == 0)
    def _():
        for rel, shift in enumerate((0, 3, 1, 2)):
            zh = lax.rem(x + shift, 4)
            for r in range(16):
                src_z = zh * 2 + r // 8
                src_y = (r // 2) % 4
                src_c = r % 2
                dz = lax.rem(z + 8 - src_z, 8)
                dy = lax.rem(y + 4 - src_y, 4)
                same = c == src_c
                p0 = pay0_ref[dy * 8 + dz]
                p1 = pay1_ref[dy * 8 + dz]
                p = jnp.where(same, p0, p1)
                for h in range(HEADS):
                    bias[h, r * ROWS : (r + 1) * ROWS, rel * LANES : (rel + 1) * LANES] = p[
                        h * ROWS : (h + 1) * ROWS
                    ]
                    row = HEADS * ROWS + (h % 2) * ROWS
                    lane = 4 * LANES + rel * HALF
                    bias[h, r * ROWS : (r + 1) * ROWS, lane : lane + HALF] = p[
                        row : row + ROWS, (h // 2) * HALF : (h // 2 + 1) * HALF
                    ]

    own = own_ref[0]
    far = jnp.where(i < ROWS // 2, far_a_ref[0], far_b_ref[0])
    four = (own, prev_ref[0], next_ref[0], far)
    keys_in = jnp.concatenate([f[:LANES] for f in four] + [f[LANES:] for f in four], axis=0)
    qg = dot(own, wqg_ref[...], NN)
    q = (qg[:, :CH] * HD ** (-0.5)).astype(BF)
    gate = jax.nn.sigmoid(qg[:, CH:])
    kv = dot(keys_in, wkv_ref[...], NN).astype(BF)
    k = kv[:, :CH]
    v1 = jnp.concatenate([kv[:, CH:], jnp.ones((4 * COLS, CH), BF)], axis=1)
    pen = pen_ref[0]
    lane_head = lax.broadcasted_iota(jnp.int32, (COLS, CH), 1) // HD
    att = jnp.zeros((COLS, CH), F32)
    for h in range(HEADS):
        mine = lane_head == h
        qh = jnp.where(mine, q, jnp.zeros_like(q))
        s = dot(qh, k, NT) + bias[h] + pen
        p = jnp.exp(s - jnp.max(s, axis=-1, keepdims=True)).astype(BF)
        o = dot(p, v1, NN)
        att = jnp.where(mine, o[:, :CH] / o[:, CH:], att)
    gated = (gate * att).astype(BF)
    out_ref[0] = dot(gated, wo_ref[...], NN).astype(BF)


def attend(pos, own, prev, nxt, far_a, far_b, pay0, pay1, pen, wqg, wkv, wo):
    vmem = pl.BlockSpec(memory_space=pltpu.VMEM)
    row = lambda f: pl.BlockSpec((1, COLS, CH), lambda i: (f(i), 0, 0))
    half = ROWS // 2
    return pl.pallas_call(
        attend_kernel,
        grid=(ROWS,),
        out_shape=jax.ShapeDtypeStruct((ROWS, COLS, CH), BF),
        in_specs=[
            pl.BlockSpec(memory_space=pltpu.SMEM),
            row(lambda i: i), row(lambda i: i), row(lambda i: i),
            row(lambda i: jnp.minimum(i, half - 1)), row(lambda i: jnp.maximum(i - half, 0)),
            vmem, vmem,
            pl.BlockSpec((1, 1, 4 * COLS), lambda i: (i, 0, 0)),
            vmem, vmem, vmem,
        ],
        out_specs=row(lambda i: i),
        scratch_shapes=[pltpu.VMEM((HEADS, COLS, 4 * COLS), F32)],
        compiler_params=pltpu.CompilerParams(vmem_limit_bytes=56 * 1024 * 1024),
        cost_estimate=pl.CostEstimate(flops=8 * 10**9, bytes_accessed=10**7, transcendentals=7 * 10**6),
        name="attend",
    )(pos, own, prev, nxt, far_a, far_b, pay0, pay1, pen, wqg, wkv, wo)


def standardise_features(values):
    widened = values.astype(F32)
    centered = widened - jnp.mean(widened, axis=-1, keepdims=True)
    spread = jnp.mean(centered * centered, axis=-1, keepdims=True)
    return centered * lax.rsqrt(spread + 1e-05)


ALL = ("zh", "zl", "y", "c", "x")
SWAP = [
    ((a * 16 + r) * 4 + b, (b * 16 + r) * 4 + a) for a in range(4) for r in range(16) for b in range(4)
]


def gather_right(own):
    pp = lax.ppermute
    z = pp(own, "zl", ring(2, 1))
    up, down = pp(own, "y", ring(4, 1)), pp(own, "y", ring(4, 3))
    zup, zdown = pp(z, "y", ring(4, 1)), pp(z, "y", ring(4, 3))
    h = BLK // 2
    far_a, far_b = pp(up[:h], "y", ring(4, 1)), pp(down[h:], "y", ring(4, 3))
    zfar_a, zfar_b = pp(zup[:h], "y", ring(4, 1)), pp(zdown[h:], "y", ring(4, 3))
    mine = [own, z, up, down, zup, zdown, far_a, far_b, zfar_a, zfar_b]
    return mine + [pp(m, "c", ring(2, 1)) for m in mine]


def gather_bias(own):
    pp = lax.ppermute
    zz = ("zh", "zl")
    up, down = [own], [own]
    for _ in range(3):
        up.append(pp(up[-1], zz, ring(8, 1)))
        down.append(pp(down[-1], zz, ring(8, 7)))
    h = 40
    last_a = pp(up[-1][:h], zz, ring(8, 1))
    last_b = pp(down[-1][h:], zz, ring(8, 7))
    last = jnp.concatenate([last_a, last_b], axis=0)
    col = jnp.stack([own, up[1], up[2], up[3], last, down[3], down[2], down[1]])
    yup, ydown = pp(col, "y", ring(4, 1)), pp(col, "y", ring(4, 3))
    far_a, far_b = pp(yup[:4], "y", ring(4, 1)), pp(ydown[4:], "y", ring(4, 3))
    full = jnp.concatenate([col, yup, far_a, far_b, ydown], axis=0)
    return full, pp(full, "c", ring(2, 1))


def body(stack, emb, entry, final, qkg, offset, out_proj, filt):
    pp = lax.ppermute
    zh, zl = lax.axis_index("zh"), lax.axis_index("zl")
    y, c, x = lax.axis_index("y"), lax.axis_index("c"), lax.axis_index("x")
    normed = standardise_features(stack).astype(BF)
    proj = jnp.einsum("sjc,cx->jxs", normed, entry, preferred_element_type=F32).astype(BF)
    left = proj[:, :PF].reshape(BLK, MSA)
    right = proj[:, PF:].reshape(BLK, MSA)
    pieces = gather_right(pp(right, ALL, SWAP))

    w = final.reshape(PF, PF, CH).transpose(1, 0, 2)
    eye = jnp.eye(4, dtype=BF)
    wblk = (w[:, None, :, None, :] * eye[None, :, None, :, None]).reshape(PF * LANES, 4 * CH)
    off = jnp.pad(offset.T, ((0, 4), (0, 0)))
    pos_a = jnp.stack([zl, y, c]).astype(jnp.int32)
    mid, norm, bias = opm(pos_a, left, pieces, wblk, emb, off)

    prev, nxt = pp(norm, "x", ring(4, 1)), pp(norm, "x", ring(4, 3))
    half = ROWS // 2
    far_a, far_b = pp(prev[:half], "x", ring(4, 1)), pp(nxt[half:], "x", ring(4, 3))
    pay0, pay1 = gather_bias(pp(bias, ALL, SWAP))

    tiles = filt.shape[0]
    tile = 4 * COLS // tiles
    rows = (zh * 16 + zl * 8 + y * 2 + c) * ROWS + jnp.arange(ROWS)
    slots = lax.rem(x + jnp.array([0, 3, 1, 2]), 4) * COLS
    cols = jnp.concatenate(
        [
            (slots[:, None] + jnp.arange(LANES)[None]).reshape(-1),
            (slots[:, None] + LANES + jnp.arange(HALF)[None]).reshape(-1),
        ]
    )
    pick = lambda idx: (idx[:, None] // tile == jnp.arange(tiles)[None, :]).astype(F32)
    keep = jnp.einsum(
        "it,tu,ku->ik", pick(rows), filt.astype(F32), pick(cols), precision=lax.Precision.HIGHEST
    )
    pen = ((keep - 1.0) * 1000000000.0)[:, None, :]
    pos_b = jnp.stack([zh * 2 + zl, y, c, x]).astype(jnp.int32)
    wqg = jnp.concatenate([qkg[:, :CH], qkg[:, 3 * CH :]], axis=1)
    wkv = qkg[:, CH : 3 * CH]
    update = attend(pos_b, norm, prev, nxt, far_a, far_b, pay0, pay1, pen, wqg, wkv, out_proj)
    return mid, update


def solution(mesh):
    fine = jax.sharding.Mesh(mesh.devices.reshape(4, 2, 4, 2, 4), ALL)
    dap = ("zh", "zl", "y", "c")
    in_specs = (P(None, dap, None), P(dap, "x", None), P(), P(), P(), P(), P(), P())
    out_specs = (P(dap, "x", None), P(dap, "x", None))
    return jax.shard_map(body, mesh=fine, in_specs=in_specs, out_specs=out_specs, check_vma=False)
```

```python
import jax
import jax.numpy as jnp
from jax import lax
from jax.experimental import pallas as pl
from jax.experimental.pallas import tpu as pltpu
from jax.sharding import PartitionSpec as P

BF = jnp.bfloat16
F32 = jnp.float32
NT = (((1,), (1,)), ((), ()))
NN = (((1,), (0,)), ((), ()))

ROWS, COLS, CH, HEADS, HD = 12, 192, 128, 4, 32
MSA, PF = 256, 32
BLK = ROWS * PF
LANES = 128
HALF = COLS - LANES
PAY = HEADS * ROWS
LOG2E = 1.4426950408889634
TILES, TILE = 6, 128


def ring(n, k):
    return [(i, (i + k) % n) for i in range(n)]


def dot(a, b, dims):
    return lax.dot_general(a, b, dims, preferred_element_type=F32)


PIECES = [
    (z, y, c) for c in range(2) for (z, y) in ((0, 0), (1, 0), (0, 1), (0, 3), (0, 2), (1, 1), (1, 3), (1, 2))
]


def by_channel(res, lhs, t):
    low = lax.broadcasted_iota(jnp.int32, (PF // 2, 8, LANES), 1) < 4
    for q in range(3):
        part = res[:, q * LANES : (q + 1) * LANES]
        tiles = []
        for k in range(2):
            a, b = [], []
            for c in range(2):
                base = (2 * k + c) * BLK
                a.append(part[base : base + 8 * PF].reshape(PF, 8, LANES))
                b.append(part[base + 8 * PF : base + BLK].reshape(PF // 2, 8, LANES))
            even = jnp.where(low, b[0], jnp.roll(b[1], 4, axis=1))
            odd = jnp.where(low, jnp.roll(b[0], 4, axis=1), b[1])
            tiles.append((a[0], a[1], (even, odd)))
        rows = pl.multiple_of(q * COLS + t * 4 * ROWS, 16)
        for ch in range(PF):
            six = []
            for a0, a1, eo in tiles:
                six += [a0[ch], a1[ch], eo[ch % 2][ch // 2]]
            lhs[pl.ds(rows, 4 * ROWS), ch * LANES : (ch + 1) * LANES] = jnp.concatenate(six, axis=0).astype(BF)


def natural(acc):
    n = acc.shape[1]
    p = acc.reshape(8, 3, 8, n)
    low = lax.broadcasted_iota(jnp.int32, (8, 8, n), 1) < 4
    r = jnp.roll(p[:, 1], 4, axis=1)
    mid = jnp.where(low, p[:, 2], r)
    last = jnp.where(low, r, p[:, 2])
    return jnp.concatenate([p[:, 0:1], mid[:, None], last[:, None]], axis=1).reshape(COLS, n)


def opm_kernel(pos_ref, lt_ref, *refs):
    pieces = refs[: len(PIECES)]
    (w_ref, emb_ref, off_ref, mid_ref, norm_ref, bias_ref) = refs[len(PIECES) : len(PIECES) + 6]
    (right, lhs, wblk, brow, sems) = refs[len(PIECES) + 6 :]
    zl, y, c = pos_ref[0], pos_ref[1], pos_ref[2]
    copies = []
    for n, (dz, dy, dc) in enumerate(PIECES):
        src_z = lax.rem(zl + dz, 2)
        src_y = lax.rem(y + 4 - dy, 4)
        src_c = lax.rem(c + dc, 2)
        start = (src_z * 8 + src_y * 2 + src_c) * BLK
        cp = pltpu.make_async_copy(
            pieces[n], right.at[pl.ds(pl.multiple_of(start, 128), BLK)], sems.at[n]
        )
        cp.start()
        copies.append(cp)

    def build(ch, carry):
        base = pl.multiple_of(ch * LANES, LANES)
        wy = w_ref[ch]
        zero = jnp.zeros((PF, CH), BF)
        for r in range(4):
            for t in range(4):
                wblk[pl.ds(base + r * PF, PF), t * CH : (t + 1) * CH] = wy if r == t else zero
        return carry

    lax.fori_loop(0, PF, build, 0)
    for cp in copies:
        cp.wait()

    def first(t, carry):
        rows = pl.multiple_of(t * 4 * BLK, 4 * BLK)
        by_channel(dot(right[pl.ds(rows, 4 * BLK), :], lt_ref[...], NT), lhs, t)
        return carry

    lax.fori_loop(0, 4, first, 0)
    w = off_ref[...]
    w_hi = w.astype(BF)
    rest = w - w_hi.astype(F32)
    w_mid = rest.astype(BF)
    w_lo = (rest - w_mid.astype(F32)).astype(BF)
    w3 = jnp.concatenate([w_hi, w_mid, w_lo], axis=0)
    for q in range(3):
        update = natural(dot(lhs[q * COLS : (q + 1) * COLS, :], wblk[...], NN)) * (1.0 / MSA)
        for r in range(4):
            i = 4 * q + r
            mid = (emb_ref[i].astype(F32) + update[:, r * CH : (r + 1) * CH]).astype(BF)
            mid_ref[i] = mid
            wide = mid.astype(F32)
            cen = wide - jnp.mean(wide, axis=-1, keepdims=True)
            var = jnp.mean(cen * cen, axis=-1, keepdims=True)
            nrm = (cen * lax.rsqrt(var + 1e-05)).astype(BF)
            norm_ref[i] = nrm
            parts = dot(w3, nrm, NT)
            brow[i] = parts[0:8] + parts[8:16] + parts[16:24]
    for h in range(HEADS):
        b = brow[:, h, :]
        done = []
        tops = []
        for g in range(3):
            part = b[:, g * HALF : (g + 1) * HALF]
            top = jnp.max(part, axis=-1, keepdims=True).astype(BF).astype(F32)
            done.append(part - top)
            tops.append(top)
        lane = lax.broadcasted_iota(jnp.int32, (ROWS, HALF), 1)
        tail = jnp.where(lane == 0, tops[0], jnp.where(lane == 1, tops[1], tops[2]))
        bias_ref[h * ROWS : (h + 1) * ROWS, :] = jnp.concatenate(done + [tail], axis=1).astype(BF)


VMEM = pl.BlockSpec(memory_space=pltpu.VMEM)
SMEM = pl.BlockSpec(memory_space=pltpu.SMEM)
ANY = pl.BlockSpec(memory_space=pl.ANY)
PARAMS = pltpu.CompilerParams(vmem_limit_bytes=56 * 1024 * 1024)


def opm(pos, left, pieces, w, emb, off):
    return pl.pallas_call(
        opm_kernel,
        out_shape=(
            jax.ShapeDtypeStruct((ROWS, COLS, CH), BF),
            jax.ShapeDtypeStruct((ROWS, COLS, CH), BF),
            jax.ShapeDtypeStruct((PAY, 2 * LANES), BF),
        ),
        in_specs=[SMEM, VMEM] + [ANY] * len(PIECES) + [VMEM] * 3,
        out_specs=[VMEM] * 3,
        scratch_shapes=[
            pltpu.VMEM((16 * BLK, MSA), BF),
            pltpu.VMEM((3 * COLS, PF * LANES), BF),
            pltpu.VMEM((PF * LANES, 4 * CH), BF),
            pltpu.VMEM((ROWS, 8, COLS), F32),
            pltpu.SemaphoreType.DMA((len(PIECES),)),
        ],
        compiler_params=PARAMS,
        cost_estimate=pl.CostEstimate(flops=6 * 10**9, bytes_accessed=10**7, transcendentals=0),
        name="opm",
    )(pos, left, *pieces, w, emb, off)


def attend_kernel(
    pos_ref, filt_ref, own_ref, prev_ref, next_ref, far_ref, pay0_ref, pay1_ref,
    wqg_ref, wkv_ref, wo_ref, out_ref, bias,
):
    i = pl.program_id(0)
    z, y, c, x = pos_ref[0], pos_ref[1], pos_ref[2], pos_ref[3]

    @pl.when(i == 0)
    def _():
        first_lane = lax.broadcasted_iota(jnp.int32, (PAY, LANES), 1) < HALF

        def place(pair, carry):
            row0 = pl.multiple_of(pair * 2 * ROWS, 8)
            src_z = pair // 4
            src_y = lax.rem(pair, 4)
            dy = lax.rem(y + 4 - src_y, 4)
            tails = []
            for rel, shift in enumerate((0, 3, 1, 2)):
                zh = lax.rem(x + shift, 4)
                dz = lax.rem(z + 8 - zh * 2 - src_z, 8)
                at = dy * 8 + dz
                p0 = pay0_ref[at].astype(F32) * LOG2E
                p1 = pay1_ref[at].astype(F32) * LOG2E
                heads = []
                for p in (jnp.where(c == 0, p0, p1), jnp.where(c == 0, p1, p0)):
                    m = COLS
                    heads.append(
                        p[:, :LANES] + jnp.where(first_lane, p[:, m : m + 1], p[:, m + 1 : m + 2])
                    )
                    tails.append(p[:, LANES:COLS] + p[:, m + 2 : m + 3])
                for h in range(HEADS):
                    cut = slice(h * ROWS, (h + 1) * ROWS)
                    bias[h, pl.ds(row0, 2 * ROWS), rel * LANES : (rel + 1) * LANES] = jnp.concatenate(
                        [heads[0][cut], heads[1][cut]], axis=0
                    )
            for half in range(2):
                t = tails[4 * half : 4 * half + 4]
                both = [jnp.concatenate([t[0], t[2]], axis=1), jnp.concatenate([t[1], t[3]], axis=1)]
                lane = (4 + half) * LANES
                for h in range(HEADS):
                    cut = slice(h * ROWS, (h + 1) * ROWS)
                    bias[h, pl.ds(row0, 2 * ROWS), lane : lane + LANES] = jnp.concatenate(
                        [both[0][cut], both[1][cut]], axis=0
                    )
            return carry

        lax.fori_loop(0, 8, place, 0)

    own = own_ref[0]
    four = (own, prev_ref[0], next_ref[0], far_ref[0])
    keys_in = jnp.concatenate([f[:LANES] for f in four] + [f[LANES:] for f in four], axis=0)
    qg = dot(own, wqg_ref[...], NN)
    q = (qg[:, :CH] * (HD ** (-0.5) * LOG2E)).astype(BF)
    gate = jax.nn.sigmoid(qg[:, CH:])
    kv = dot(keys_in, wkv_ref[...], NN).astype(BF)
    k = kv[:, :CH]
    v1 = jnp.concatenate([kv[:, CH:], jnp.ones((4 * COLS, CH), BF)], axis=1)
    row_tile = (pos_ref[4] + i) // TILE
    run = lax.broadcasted_iota(jnp.int32, (1, 4 * COLS), 1) // HALF
    pen = jnp.zeros((1, 4 * COLS), F32)
    for rel, shift in enumerate((0, 3, 1, 2)):
        col = lax.rem(x + shift, 4) * COLS
        for slot, start in ((2 * rel, 0), (2 * rel + 1, HALF), (8 + rel, LANES)):
            keep = filt_ref[row_tile * TILES + (col + start) // TILE]
            pen = jnp.where(run == slot, (keep.astype(F32) - 1.0) * 1000000000.0, pen)
    lane_head = lax.broadcasted_iota(jnp.int32, (COLS, CH), 1) // HD
    att = jnp.zeros((COLS, CH), F32)
    for h in range(HEADS):
        mine = lane_head == h
        qh = jnp.where(mine, q, jnp.zeros_like(q))
        s = dot(qh, k, NT) + bias[h] + pen
        p = jnp.exp2(s - jnp.max(s, axis=-1, keepdims=True)).astype(BF)
        o = dot(p, v1, NN)
        att = jnp.where(mine, o[:, :CH] / o[:, CH:], att)
    gated = (gate * att).astype(BF)
    out_ref[0] = dot(gated, wo_ref[...], NN).astype(BF)


def attend(pos, filt, own, prev, nxt, far, pay0, pay1, wqg, wkv, wo):
    row = pl.BlockSpec((1, COLS, CH), lambda i: (i, 0, 0))
    return pl.pallas_call(
        attend_kernel,
        grid=(ROWS,),
        out_shape=jax.ShapeDtypeStruct((ROWS, COLS, CH), BF),
        in_specs=[SMEM, SMEM] + [row] * 4 + [VMEM] * 5,
        out_specs=row,
        scratch_shapes=[pltpu.VMEM((HEADS, COLS, 4 * COLS), F32)],
        compiler_params=PARAMS,
        cost_estimate=pl.CostEstimate(flops=8 * 10**9, bytes_accessed=10**7, transcendentals=7 * 10**6),
        name="attend",
    )(pos, filt, own, prev, nxt, far, pay0, pay1, wqg, wkv, wo)


def standardise_features(values):
    widened = values.astype(F32)
    centered = widened - jnp.mean(widened, axis=-1, keepdims=True)
    spread = jnp.mean(centered * centered, axis=-1, keepdims=True)
    return centered * lax.rsqrt(spread + 1e-05)


ALL = ("zh", "zl", "y", "c", "x")
SWAP = [
    ((a * 16 + r) * 4 + b, (b * 16 + r) * 4 + a) for a in range(4) for r in range(16) for b in range(4)
]


def gather_right(own):
    pp = lax.ppermute
    z = pp(own, "zl", ring(2, 1))
    up, down, far = [pp(own, "y", ring(4, k)) for k in (1, 3, 2)]
    zup, zdown = pp(z, "y", ring(4, 1)), pp(z, "y", ring(4, 3))
    zfar = pp(far, "zl", ring(2, 1))
    mine = [own, z, up, down, far, zup, zdown, zfar]
    return mine + [pp(m, "c", ring(2, 1)) for m in mine]


def gather_bias_z(own):
    pp = lax.ppermute
    zz = ("zh", "zl")
    up, down = pp(own, zz, ring(8, 1)), pp(own, zz, ring(8, 7))
    ahead = pp(jnp.stack([down, own, up]), zz, ring(8, 3))
    behind = pp(jnp.stack([down, own, up][1:]), zz, ring(8, 5))
    return jnp.concatenate([own[None], up[None], ahead, behind, down[None]], axis=0)


def gather_bias_y(col):
    up, down, far = [lax.ppermute(col, "y", ring(4, k)) for k in (1, 3, 2)]
    return jnp.concatenate([col, up, far, down], axis=0)


def body(stack, emb, entry, final, qkg, offset, out_proj, filt):
    pp = lax.ppermute
    zh, zl = lax.axis_index("zh"), lax.axis_index("zl")
    y, c, x = lax.axis_index("y"), lax.axis_index("c"), lax.axis_index("x")
    normed = standardise_features(stack).astype(BF)
    proj = jnp.einsum("sjc,cx->jxs", normed, entry, preferred_element_type=F32).astype(BF)
    left = proj[:, :PF].reshape(BLK, MSA)
    right = proj[:, PF:].transpose(1, 0, 2)
    right = jnp.concatenate([right[:, :8].reshape(8 * PF, MSA), right[:, 8:].reshape(4 * PF, MSA)], axis=0)
    pieces = gather_right(pp(right, ALL, SWAP))
    w = final.reshape(PF, PF, CH).transpose(1, 0, 2)
    off = jnp.pad(offset.T, ((0, 4), (0, 0)))
    pos_a = jnp.stack([zl, y, c]).astype(jnp.int32)
    mid, norm, bias = opm(pos_a, left, pieces, w, emb, off)
    prev, nxt, far = [pp(norm, "x", ring(4, k)) for k in (1, 3, 2)]
    col = gather_bias_z(pp(bias, ALL, SWAP))
    wqg = jnp.concatenate([qkg[:, :CH], qkg[:, 3 * CH :]], axis=1)
    pay0 = gather_bias_y(col)
    prev, nxt, far, pay0 = lax.optimization_barrier((prev, nxt, far, pay0))
    pay1 = pp(pay0, "c", ring(2, 1))

    row0 = (zh * 16 + zl * 8 + y * 2 + c) * ROWS
    pos_b = jnp.stack([zh * 2 + zl, y, c, x, row0]).astype(jnp.int32)
    wkv = qkg[:, CH : 3 * CH]
    update = attend(pos_b, filt.reshape(-1), norm, prev, nxt, far, pay0, pay1, wqg, wkv, out_proj)
    return mid, update


def solution(mesh):
    fine = jax.sharding.Mesh(mesh.devices.reshape(4, 2, 4, 2, 4), ALL)
    dap = ("zh", "zl", "y", "c")
    in_specs = (P(None, dap, None), P(dap, "x", None), P(), P(), P(), P(), P(), P())
    out_specs = (P(dap, "x", None), P(dap, "x", None))
    return jax.shard_map(body, mesh=fine, in_specs=in_specs, out_specs=out_specs, check_vma=False)
```

```python
import jax
import jax.numpy as jnp
from jax import lax
from jax.experimental import pallas as pl
from jax.experimental.pallas import tpu as pltpu
from jax.sharding import PartitionSpec as P

BF = jnp.bfloat16
F32 = jnp.float32
NT = (((1,), (1,)), ((), ()))
NN = (((1,), (0,)), ((), ()))

ROWS, COLS, CH, HEADS, HD = 12, 192, 128, 4, 32
MSA, PF = 256, 32
BLK = ROWS * PF
LANES = 128
HALF = COLS - LANES
PAY = HEADS * ROWS
LOG2E = 1.4426950408889634
TILE = 128


def ring(n, k):
    return [(i, (i + k) % n) for i in range(n)]


def dot(a, b, dims):
    return lax.dot_general(a, b, dims, preferred_element_type=F32)


PIECES = [
    (z, y, c) for c in range(2) for (z, y) in ((0, 0), (1, 0), (0, 1), (0, 3), (0, 2), (1, 1), (1, 3), (1, 2))
]


def by_channel(res, lhs, t):
    low = lax.broadcasted_iota(jnp.int32, (PF // 2, 8, LANES), 1) < 4
    for q in range(3):
        part = res[:, q * LANES : (q + 1) * LANES]
        tiles = []
        for k in range(2):
            a, b = [], []
            for c in range(2):
                base = (2 * k + c) * BLK
                a.append(part[base : base + 8 * PF].reshape(PF, 8, LANES))
                b.append(part[base + 8 * PF : base + BLK].reshape(PF // 2, 8, LANES))
            even = jnp.where(low, b[0], jnp.roll(b[1], 4, axis=1))
            odd = jnp.where(low, jnp.roll(b[0], 4, axis=1), b[1])
            tiles.append((a[0], a[1], (even, odd)))
        rows = pl.multiple_of(q * COLS + t * 4 * ROWS, 16)
        for ch in range(PF):
            six = []
            for a0, a1, eo in tiles:
                six += [a0[ch], a1[ch], eo[ch % 2][ch // 2]]
            lhs[pl.ds(rows, 4 * ROWS), ch * LANES : (ch + 1) * LANES] = jnp.concatenate(six, axis=0).astype(BF)


def natural(acc):
    n = acc.shape[1]
    p = acc.reshape(8, 3, 8, n)
    low = lax.broadcasted_iota(jnp.int32, (8, 8, n), 1) < 4
    r = jnp.roll(p[:, 1], 4, axis=1)
    mid = jnp.where(low, p[:, 2], r)
    last = jnp.where(low, r, p[:, 2])
    return jnp.concatenate([p[:, 0:1], mid[:, None], last[:, None]], axis=1).reshape(COLS, n)


def opm_kernel(pos_ref, lt_ref, *refs):
    pieces = refs[: len(PIECES)]
    (w_ref, emb_ref, off_ref, mid_ref, norm_ref, bias_ref) = refs[len(PIECES) : len(PIECES) + 6]
    (right, lhs, wblk, brow, sems) = refs[len(PIECES) + 6 :]
    zl, y, c = pos_ref[0], pos_ref[1], pos_ref[2]
    copies = []
    for n, (dz, dy, dc) in enumerate(PIECES):
        src_z = lax.rem(zl + dz, 2)
        src_y = lax.rem(y + 4 - dy, 4)
        src_c = lax.rem(c + dc, 2)
        start = (src_z * 8 + src_y * 2 + src_c) * BLK
        cp = pltpu.make_async_copy(
            pieces[n], right.at[pl.ds(pl.multiple_of(start, 128), BLK)], sems.at[n]
        )
        cp.start()
        copies.append(cp)

    def build(ch, carry):
        base = pl.multiple_of(ch * LANES, LANES)
        wy = w_ref[ch]
        zero = jnp.zeros((PF, CH), BF)
        for r in range(4):
            for t in range(4):
                wblk[pl.ds(base + r * PF, PF), t * CH : (t + 1) * CH] = wy if r == t else zero
        return carry

    lax.fori_loop(0, PF, build, 0)
    for cp in copies:
        cp.wait()

    def first(t, carry):
        rows = pl.multiple_of(t * 4 * BLK, 4 * BLK)
        by_channel(dot(right[pl.ds(rows, 4 * BLK), :], lt_ref[...], NT), lhs, t)
        return carry

    lax.fori_loop(0, 4, first, 0)
    w = off_ref[...]
    w_hi = w.astype(BF)
    rest = w - w_hi.astype(F32)
    w_mid = rest.astype(BF)
    w_lo = (rest - w_mid.astype(F32)).astype(BF)
    w3 = jnp.concatenate([w_hi, w_mid, w_lo], axis=0)
    for q in range(3):
        update = natural(dot(lhs[q * COLS : (q + 1) * COLS, :], wblk[...], NN)) * (1.0 / MSA)
        for r in range(4):
            i = 4 * q + r
            mid = (emb_ref[i].astype(F32) + update[:, r * CH : (r + 1) * CH]).astype(BF)
            mid_ref[i] = mid
            wide = mid.astype(F32)
            cen = wide - jnp.mean(wide, axis=-1, keepdims=True)
            var = jnp.mean(cen * cen, axis=-1, keepdims=True)
            nrm = (cen * lax.rsqrt(var + 1e-05)).astype(BF)
            norm_ref[i] = nrm
            parts = dot(w3, nrm, NT)
            brow[i] = parts[0:8] + parts[8:16] + parts[16:24]
    for h in range(HEADS):
        b = brow[:, h, :]
        done = []
        tops = []
        for g in range(3):
            part = b[:, g * HALF : (g + 1) * HALF]
            top = jnp.max(part, axis=-1, keepdims=True).astype(BF).astype(F32)
            done.append(part - top)
            tops.append(top)
        lane = lax.broadcasted_iota(jnp.int32, (ROWS, HALF), 1)
        tail = jnp.where(lane == 0, tops[0], jnp.where(lane == 1, tops[1], tops[2]))
        bias_ref[h * ROWS : (h + 1) * ROWS, :] = jnp.concatenate(done + [tail], axis=1).astype(BF)


VMEM = pl.BlockSpec(memory_space=pltpu.VMEM)
SMEM = pl.BlockSpec(memory_space=pltpu.SMEM)
ANY = pl.BlockSpec(memory_space=pl.ANY)
PARAMS = pltpu.CompilerParams(vmem_limit_bytes=56 * 1024 * 1024)


def opm(pos, left, pieces, w, emb, off):
    return pl.pallas_call(
        opm_kernel,
        out_shape=(
            jax.ShapeDtypeStruct((ROWS, COLS, CH), BF),
            jax.ShapeDtypeStruct((ROWS, COLS, CH), BF),
            jax.ShapeDtypeStruct((PAY, 2 * LANES), BF),
        ),
        in_specs=[SMEM, VMEM] + [ANY] * len(PIECES) + [VMEM] * 3,
        out_specs=[VMEM] * 3,
        scratch_shapes=[
            pltpu.VMEM((16 * BLK, MSA), BF),
            pltpu.VMEM((3 * COLS, PF * LANES), BF),
            pltpu.VMEM((PF * LANES, 4 * CH), BF),
            pltpu.VMEM((ROWS, 8, COLS), F32),
            pltpu.SemaphoreType.DMA((len(PIECES),)),
        ],
        compiler_params=PARAMS,
        cost_estimate=pl.CostEstimate(flops=6 * 10**9, bytes_accessed=10**7, transcendentals=0),
        name="opm",
    )(pos, left, *pieces, w, emb, off)


def project_kernel(own_ref, prev_ref, next_ref, far_ref, qkg_ref, q_ref, gate_ref, kv_ref):
    own = own_ref[0]
    four = (own, prev_ref[0], next_ref[0], far_ref[0])
    keys_in = jnp.concatenate([f[:LANES] for f in four] + [f[LANES:] for f in four], axis=0)
    q_ref[0] = (dot(own, qkg_ref[:, :CH], NN) * (HD ** (-0.5) * LOG2E)).astype(BF)
    gate_ref[0] = jax.nn.sigmoid(dot(own, qkg_ref[:, 3 * CH :], NN))
    kv_ref[0] = dot(keys_in, qkg_ref[:, CH : 3 * CH], NN).astype(BF)


def project(own, prev, nxt, far, qkg):
    row = pl.BlockSpec((1, COLS, CH), lambda i: (i, 0, 0))
    return pl.pallas_call(
        project_kernel,
        grid=(ROWS,),
        out_shape=(
            jax.ShapeDtypeStruct((ROWS, COLS, CH), BF),
            jax.ShapeDtypeStruct((ROWS, COLS, CH), F32),
            jax.ShapeDtypeStruct((ROWS, 4 * COLS, 2 * CH), BF),
        ),
        in_specs=[row] * 4 + [VMEM],
        out_specs=[row, row, pl.BlockSpec((1, 4 * COLS, 2 * CH), lambda i: (i, 0, 0))],
        compiler_params=PARAMS,
        cost_estimate=pl.CostEstimate(flops=10**10, bytes_accessed=2 * 10**7, transcendentals=10**5),
        name="project",
    )(own, prev, nxt, far, qkg)


def attend_kernel(
    pos_ref, filt_ref, q_ref, gate_ref, kv_ref, pay0_ref, pay1_ref, wo_ref, out_ref, bias,
):
    i = pl.program_id(0)
    c, zh, x = pos_ref[2], pos_ref[3], pos_ref[4]

    @pl.when(i == 0)
    def _():
        first_lane = lax.broadcasted_iota(jnp.int32, (PAY, LANES), 1) < HALF

        def place(pair, carry):
            row0 = pl.multiple_of(pair * 2 * ROWS, 8)
            tails = []
            for rel, shift in enumerate((0, 3, 1, 2)):
                at = lax.rem(zh + 8 - x - shift, 4)
                p0 = pay0_ref[pair, at].astype(F32) * LOG2E
                p1 = pay1_ref[pair, at].astype(F32) * LOG2E
                heads = []
                for p in (jnp.where(c == 0, p0, p1), jnp.where(c == 0, p1, p0)):
                    m = COLS
                    heads.append(
                        p[:, :LANES] + jnp.where(first_lane, p[:, m : m + 1], p[:, m + 1 : m + 2])
                    )
                    tails.append(p[:, LANES:COLS] + p[:, m + 2 : m + 3])
                for h in range(HEADS):
                    cut = slice(h * ROWS, (h + 1) * ROWS)
                    bias[h, pl.ds(row0, 2 * ROWS), rel * LANES : (rel + 1) * LANES] = jnp.concatenate(
                        [heads[0][cut], heads[1][cut]], axis=0
                    )
            for half in range(2):
                t = tails[4 * half : 4 * half + 4]
                both = [jnp.concatenate([t[0], t[2]], axis=1), jnp.concatenate([t[1], t[3]], axis=1)]
                lane = (4 + half) * LANES
                for h in range(HEADS):
                    cut = slice(h * ROWS, (h + 1) * ROWS)
                    bias[h, pl.ds(row0, 2 * ROWS), lane : lane + LANES] = jnp.concatenate(
                        [both[0][cut], both[1][cut]], axis=0
                    )
            return carry

        lax.fori_loop(0, 8, place, 0)

    q, gate, kv = q_ref[0], gate_ref[0], kv_ref[0]
    k = kv[:, :CH]
    v1 = jnp.concatenate([kv[:, CH:], jnp.ones((4 * COLS, CH), BF)], axis=1)
    row_tile = (pos_ref[5] + i) // TILE
    run = lax.broadcasted_iota(jnp.int32, (1, 4 * COLS), 1) // HALF
    pen = jnp.zeros((1, 4 * COLS), F32)
    for rel, shift in enumerate((0, 3, 1, 2)):
        col = lax.rem(x + shift, 4) * COLS
        for slot, start in ((2 * rel, 0), (2 * rel + 1, HALF), (8 + rel, LANES)):
            keep = filt_ref[row_tile, (col + start) // TILE]
            pen = jnp.where(run == slot, (keep.astype(F32) - 1.0) * 1000000000.0, pen)
    lane_head = lax.broadcasted_iota(jnp.int32, (COLS, CH), 1) // HD
    att = jnp.zeros((COLS, CH), F32)
    for h in range(HEADS):
        mine = lane_head == h
        qh = jnp.where(mine, q, jnp.zeros_like(q))
        s = dot(qh, k, NT) + bias[h] + pen
        p = jnp.exp2(s - jnp.max(s, axis=-1, keepdims=True)).astype(BF)
        o = dot(p, v1, NN)
        att = jnp.where(mine, o[:, :CH] / o[:, CH:], att)
    gated = (gate * att).astype(BF)
    out_ref[0] = dot(gated, wo_ref[...], NN).astype(BF)


def attend(pos, filt, q, gate, kv, pay0, pay1, wo):
    row = pl.BlockSpec((1, COLS, CH), lambda i: (i, 0, 0))
    return pl.pallas_call(
        attend_kernel,
        grid=(ROWS,),
        out_shape=jax.ShapeDtypeStruct((ROWS, COLS, CH), BF),
        in_specs=[SMEM, SMEM, row, row, pl.BlockSpec((1, 4 * COLS, 2 * CH), lambda i: (i, 0, 0))] + [VMEM] * 3,
        out_specs=row,
        scratch_shapes=[pltpu.VMEM((HEADS, COLS, 4 * COLS), F32)],
        compiler_params=PARAMS,
        cost_estimate=pl.CostEstimate(flops=8 * 10**9, bytes_accessed=10**7, transcendentals=7 * 10**6),
        name="attend",
    )(pos, filt, q, gate, kv, pay0, pay1, wo)


def standardise_features(values):
    widened = values.astype(F32)
    centered = widened - jnp.mean(widened, axis=-1, keepdims=True)
    spread = jnp.mean(centered * centered, axis=-1, keepdims=True)
    return centered * lax.rsqrt(spread + 1e-05)


ALL = ("zh", "zl", "y", "c", "x")
SWAP = [
    ((a * 16 + r) * 4 + b, (b * 16 + r) * 4 + a) for a in range(4) for r in range(16) for b in range(4)
]


SPREAD = [
    ((a * 16 + r) * 4 + (2 * a - b + 2) % 4, (b * 16 + r) * 4 + a)
    for a in range(4) for r in range(16) for b in range(4)
]


def gather_right(own):
    pp = lax.ppermute
    z = pp(own, "zl", ring(2, 1))
    up, down, far = [pp(own, "y", ring(4, k)) for k in (1, 3, 2)]
    zup, zdown = pp(z, "y", ring(4, 1)), pp(z, "y", ring(4, 3))
    zfar = pp(far, "zl", ring(2, 1))
    mine = [own, z, up, down, far, zup, zdown, zfar]
    return mine + [pp(m, "c", ring(2, 1)) for m in mine]


def gather_bias_z(own):
    return jnp.stack([own] + [lax.ppermute(own, "zh", ring(4, k)) for k in (1, 2, 3)])


def gather_bias_near(col):
    return lax.all_to_all(jnp.broadcast_to(col[None], (8,) + col.shape), ("zl", "y"), 0, 0, tiled=True)


def body(stack, emb, entry, final, qkg, offset, out_proj, filt):
    pp = lax.ppermute
    zh, zl = lax.axis_index("zh"), lax.axis_index("zl")
    y, c, x = lax.axis_index("y"), lax.axis_index("c"), lax.axis_index("x")
    normed = standardise_features(stack).astype(BF)
    proj = jnp.einsum("sjc,cx->jxs", normed, entry, preferred_element_type=F32).astype(BF)
    left = proj[:, :PF].reshape(BLK, MSA)
    right = proj[:, PF:].transpose(1, 0, 2)
    right = jnp.concatenate([right[:, :8].reshape(8 * PF, MSA), right[:, 8:].reshape(4 * PF, MSA)], axis=0)
    row0 = (zh * 16 + zl * 8 + y * 2 + c) * ROWS
    prepared = (
        final.reshape(PF, PF, CH).transpose(1, 0, 2),
        jnp.pad(offset.T, ((0, 4), (0, 0))),
        jnp.stack([zl, y, c, zh, x, row0]).astype(jnp.int32),
    )
    right, w, off, pos = lax.optimization_barrier((pp(right, ALL, SPREAD), *prepared))
    mid, norm, bias = opm(pos, left, gather_right(right), w, emb, off)

    prev, nxt, far = [pp(norm, "x", ring(4, k)) for k in (1, 3, 2)]
    col = gather_bias_z(pp(bias, ALL, SWAP))
    prev, nxt, far, col = lax.optimization_barrier((prev, nxt, far, col))
    q, gate, kv = project(norm, prev, nxt, far, qkg)
    pay0 = gather_bias_near(col)
    q, gate, kv, pay0 = lax.optimization_barrier((q, gate, kv, pay0))
    pay1 = pp(pay0, "c", ring(2, 1))
    update = attend(pos, filt, q, gate, kv, pay0, pay1, out_proj)
    return mid, update


def solution(mesh):
    fine = jax.sharding.Mesh(mesh.devices.reshape(4, 2, 4, 2, 4), ALL)
    dap = ("zh", "zl", "y", "c")
    in_specs = (P(None, dap, None), P(dap, "x", None), P(), P(), P(), P(), P(), P())
    out_specs = (P(dap, "x", None), P(dap, "x", None))
    return jax.shard_map(body, mesh=fine, in_specs=in_specs, out_specs=out_specs, check_vma=False)
```

```python
import jax
import jax.numpy as jnp
from jax import lax
from jax.experimental import pallas as pl
from jax.experimental.pallas import tpu as pltpu
from jax.sharding import PartitionSpec as P

BF = jnp.bfloat16
F32 = jnp.float32
NT = (((1,), (1,)), ((), ()))
NN = (((1,), (0,)), ((), ()))

ROWS, COLS, CH, HEADS, HD = 12, 192, 128, 4, 32
MSA, PF = 256, 32
BLK = ROWS * PF
LANES = 128
HALF = COLS - LANES
PAY = HEADS * ROWS
LOG2E = 1.4426950408889634
TILE = 128


def ring(n, k):
    return [(i, (i + k) % n) for i in range(n)]


def dot(a, b, dims):
    return lax.dot_general(a, b, dims, preferred_element_type=F32)


PIECES = [
    (z, y, c) for c in range(2) for (z, y) in ((0, 0), (1, 0), (0, 1), (0, 3), (0, 2), (1, 1), (1, 3), (1, 2))
]


def by_channel(res, lhs, t):
    low = lax.broadcasted_iota(jnp.int32, (PF // 2, 8, LANES), 1) < 4
    for q in range(3):
        part = res[:, q * LANES : (q + 1) * LANES]
        tiles = []
        for k in range(2):
            a, b = [], []
            for c in range(2):
                base = (2 * k + c) * BLK
                a.append(part[base : base + 8 * PF].reshape(PF, 8, LANES))
                b.append(part[base + 8 * PF : base + BLK].reshape(PF // 2, 8, LANES))
            even = jnp.where(low, b[0], jnp.roll(b[1], 4, axis=1))
            odd = jnp.where(low, jnp.roll(b[0], 4, axis=1), b[1])
            tiles.append((a[0], a[1], (even, odd)))
        rows = q * COLS + t * 4 * ROWS
        for ch in range(PF):
            six = []
            for a0, a1, eo in tiles:
                six += [a0[ch], a1[ch], eo[ch % 2][ch // 2]]
            lhs[rows : rows + 4 * ROWS, ch * LANES : (ch + 1) * LANES] = jnp.concatenate(six, axis=0).astype(BF)


def natural(acc):
    n = acc.shape[1]
    p = acc.reshape(8, 3, 8, n)
    low = lax.broadcasted_iota(jnp.int32, (8, 8, n), 1) < 4
    r = jnp.roll(p[:, 1], 4, axis=1)
    mid = jnp.where(low, p[:, 2], r)
    last = jnp.where(low, r, p[:, 2])
    return jnp.concatenate([p[:, 0:1], mid[:, None], last[:, None]], axis=1).reshape(COLS, n)


def opm_kernel(pos_ref, lt_ref, *refs):
    pieces = refs[: len(PIECES)]
    (w_ref, emb_ref, off_ref, mid_ref, norm_ref, bias_ref) = refs[len(PIECES) : len(PIECES) + 6]
    (right, lhs, wblk, brow, sems) = refs[len(PIECES) + 6 :]
    zl, y, c = pos_ref[0], pos_ref[1], pos_ref[2]
    copies = []
    for n, (dz, dy, dc) in enumerate(PIECES):
        src_z = lax.rem(zl + dz, 2)
        src_y = lax.rem(y + 4 - dy, 4)
        src_c = lax.rem(c + dc, 2)
        start = (src_z * 8 + src_y * 2 + src_c) * BLK
        cp = pltpu.make_async_copy(
            pieces[n], right.at[pl.ds(pl.multiple_of(start, 128), BLK)], sems.at[n]
        )
        cp.start()
        copies.append(cp)

    def build(ch, carry):
        base = pl.multiple_of(ch * LANES, LANES)
        wy = w_ref[ch]
        zero = jnp.zeros((PF, CH), BF)
        for r in range(4):
            for t in range(4):
                wblk[pl.ds(base + r * PF, PF), t * CH : (t + 1) * CH] = wy if r == t else zero
        return carry

    lax.fori_loop(0, PF, build, 0)
    for cp in copies:
        cp.wait()

    for t in range(4):
        by_channel(dot(right[t * 4 * BLK : (t + 1) * 4 * BLK, :], lt_ref[...], NT), lhs, t)
    w = off_ref[...]
    w_hi = w.astype(BF)
    rest = w - w_hi.astype(F32)
    w_mid = rest.astype(BF)
    w_lo = (rest - w_mid.astype(F32)).astype(BF)
    w3 = jnp.concatenate([w_hi, w_mid, w_lo], axis=0)
    acc = dot(lhs[...], wblk[...], NN)
    for q in range(3):
        update = natural(acc[q * COLS : (q + 1) * COLS]) * (1.0 / MSA)
        for r in range(4):
            i = 4 * q + r
            mid = (emb_ref[i].astype(F32) + update[:, r * CH : (r + 1) * CH]).astype(BF)
            mid_ref[i] = mid
            wide = mid.astype(F32)
            cen = wide - jnp.mean(wide, axis=-1, keepdims=True)
            var = jnp.mean(cen * cen, axis=-1, keepdims=True)
            nrm = (cen * lax.rsqrt(var + 1e-05)).astype(BF)
            norm_ref[i] = nrm
            parts = dot(w3, nrm, NT)
            brow[i] = parts[0:8] + parts[8:16] + parts[16:24]
    for h in range(HEADS):
        b = brow[:, h, :]
        done = []
        tops = []
        for g in range(3):
            part = b[:, g * HALF : (g + 1) * HALF]
            top = jnp.max(part, axis=-1, keepdims=True).astype(BF).astype(F32)
            done.append(part - top)
            tops.append(top)
        lane = lax.broadcasted_iota(jnp.int32, (ROWS, HALF), 1)
        tail = jnp.where(lane == 0, tops[0], jnp.where(lane == 1, tops[1], tops[2]))
        bias_ref[h * ROWS : (h + 1) * ROWS, :] = jnp.concatenate(done + [tail], axis=1).astype(BF)


VMEM = pl.BlockSpec(memory_space=pltpu.VMEM)
SMEM = pl.BlockSpec(memory_space=pltpu.SMEM)
ANY = pl.BlockSpec(memory_space=pl.ANY)
PARAMS = pltpu.CompilerParams(vmem_limit_bytes=56 * 1024 * 1024)


def opm(pos, left, pieces, w, emb, off):
    return pl.pallas_call(
        opm_kernel,
        out_shape=(
            jax.ShapeDtypeStruct((ROWS, COLS, CH), BF),
            jax.ShapeDtypeStruct((ROWS, COLS, CH), BF),
            jax.ShapeDtypeStruct((PAY, 2 * LANES), BF),
        ),
        in_specs=[SMEM, VMEM] + [ANY] * len(PIECES) + [VMEM] * 3,
        out_specs=[VMEM] * 3,
        scratch_shapes=[
            pltpu.VMEM((16 * BLK, MSA), BF),
            pltpu.VMEM((3 * COLS, PF * LANES), BF),
            pltpu.VMEM((PF * LANES, 4 * CH), BF),
            pltpu.VMEM((ROWS, 8, COLS), F32),
            pltpu.SemaphoreType.DMA((len(PIECES),)),
        ],
        compiler_params=PARAMS,
        cost_estimate=pl.CostEstimate(flops=6 * 10**9, bytes_accessed=10**7, transcendentals=0),
        name="opm",
    )(pos, left, *pieces, w, emb, off)


def project_kernel(own_ref, prev_ref, next_ref, far_ref, qkg_ref, q_ref, gate_ref, kv_ref):
    own = own_ref[0]
    four = (own, prev_ref[0], next_ref[0], far_ref[0])
    keys_in = jnp.concatenate([f[:LANES] for f in four] + [f[LANES:] for f in four], axis=0)
    q_ref[0] = (dot(own, qkg_ref[:, :CH], NN) * (HD ** (-0.5) * LOG2E)).astype(BF)
    gate_ref[0] = jax.nn.sigmoid(dot(own, qkg_ref[:, 3 * CH :], NN))
    kv_ref[0] = dot(keys_in, qkg_ref[:, CH : 3 * CH], NN).astype(BF)


def project(own, prev, nxt, far, qkg):
    row = pl.BlockSpec((1, COLS, CH), lambda i: (i, 0, 0))
    return pl.pallas_call(
        project_kernel,
        grid=(ROWS,),
        out_shape=(
            jax.ShapeDtypeStruct((ROWS, COLS, CH), BF),
            jax.ShapeDtypeStruct((ROWS, COLS, CH), F32),
            jax.ShapeDtypeStruct((ROWS, 4 * COLS, 2 * CH), BF),
        ),
        in_specs=[row] * 4 + [VMEM],
        out_specs=[row, row, pl.BlockSpec((1, 4 * COLS, 2 * CH), lambda i: (i, 0, 0))],
        compiler_params=PARAMS,
        cost_estimate=pl.CostEstimate(flops=10**10, bytes_accessed=2 * 10**7, transcendentals=10**5),
        name="project",
    )(own, prev, nxt, far, qkg)


def attend_kernel(
    pos_ref, filt_ref, q_ref, gate_ref, kv_ref, pay0_ref, pay1_ref, wo_ref, out_ref, bias,
):
    i = pl.program_id(0)
    c, zh, x = pos_ref[2], pos_ref[3], pos_ref[4]

    @pl.when(i == 0)
    def _():
        first_lane = lax.broadcasted_iota(jnp.int32, (PAY, LANES), 1) < HALF

        def place(pair, carry):
            row0 = pl.multiple_of(pair * 2 * ROWS, 8)
            tails = []
            for rel, shift in enumerate((0, 3, 1, 2)):
                at = lax.rem(zh + 8 - x - shift, 4)
                p0 = pay0_ref[pair, at].astype(F32) * LOG2E
                p1 = pay1_ref[pair, at].astype(F32) * LOG2E
                heads = []
                for p in (jnp.where(c == 0, p0, p1), jnp.where(c == 0, p1, p0)):
                    m = COLS
                    heads.append(
                        p[:, :LANES] + jnp.where(first_lane, p[:, m : m + 1], p[:, m + 1 : m + 2])
                    )
                    tails.append(p[:, LANES:COLS] + p[:, m + 2 : m + 3])
                for h in range(HEADS):
                    cut = slice(h * ROWS, (h + 1) * ROWS)
                    bias[h, pl.ds(row0, 2 * ROWS), rel * LANES : (rel + 1) * LANES] = jnp.concatenate(
                        [heads[0][cut], heads[1][cut]], axis=0
                    )
            for half in range(2):
                t = tails[4 * half : 4 * half + 4]
                both = [jnp.concatenate([t[0], t[2]], axis=1), jnp.concatenate([t[1], t[3]], axis=1)]
                lane = (4 + half) * LANES
                for h in range(HEADS):
                    cut = slice(h * ROWS, (h + 1) * ROWS)
                    bias[h, pl.ds(row0, 2 * ROWS), lane : lane + LANES] = jnp.concatenate(
                        [both[0][cut], both[1][cut]], axis=0
                    )
            return carry

        lax.fori_loop(0, 8, place, 0)

    q, gate, kv = q_ref[0], gate_ref[0], kv_ref[0]
    k = kv[:, :CH]
    v1 = jnp.concatenate([kv[:, CH:], jnp.ones((4 * COLS, CH), BF)], axis=1)
    row_tile = (pos_ref[5] + i) // TILE
    run = lax.broadcasted_iota(jnp.int32, (1, 4 * COLS), 1) // HALF
    pen = jnp.zeros((1, 4 * COLS), F32)
    for rel, shift in enumerate((0, 3, 1, 2)):
        col = lax.rem(x + shift, 4) * COLS
        for slot, start in ((2 * rel, 0), (2 * rel + 1, HALF), (8 + rel, LANES)):
            keep = filt_ref[row_tile, (col + start) // TILE]
            pen = jnp.where(run == slot, (keep.astype(F32) - 1.0) * 1000000000.0, pen)
    lane_head = lax.broadcasted_iota(jnp.int32, (COLS, CH), 1) // HD
    att = jnp.zeros((COLS, CH), F32)
    for h in range(HEADS):
        mine = lane_head == h
        qh = jnp.where(mine, q, jnp.zeros_like(q))
        s = dot(qh, k, NT) + bias[h] + pen
        p = jnp.exp2(s - jnp.max(s, axis=-1, keepdims=True)).astype(BF)
        o = dot(p, v1, NN)
        att = jnp.where(mine, o[:, :CH] / o[:, CH:], att)
    gated = (gate * att).astype(BF)
    out_ref[0] = dot(gated, wo_ref[...], NN).astype(BF)


def attend(pos, filt, q, gate, kv, pay0, pay1, wo):
    row = pl.BlockSpec((1, COLS, CH), lambda i: (i, 0, 0))
    return pl.pallas_call(
        attend_kernel,
        grid=(ROWS,),
        out_shape=jax.ShapeDtypeStruct((ROWS, COLS, CH), BF),
        in_specs=[SMEM, SMEM, row, row, pl.BlockSpec((1, 4 * COLS, 2 * CH), lambda i: (i, 0, 0))] + [VMEM] * 3,
        out_specs=row,
        scratch_shapes=[pltpu.VMEM((HEADS, COLS, 4 * COLS), F32)],
        compiler_params=PARAMS,
        cost_estimate=pl.CostEstimate(flops=8 * 10**9, bytes_accessed=10**7, transcendentals=7 * 10**6),
        name="attend",
    )(pos, filt, q, gate, kv, pay0, pay1, wo)


def standardise_features(values):
    widened = values.astype(F32)
    centered = widened - jnp.mean(widened, axis=-1, keepdims=True)
    spread = jnp.mean(centered * centered, axis=-1, keepdims=True)
    return centered * lax.rsqrt(spread + 1e-05)


ALL = ("zh", "zl", "y", "c", "x")
SWAP = [
    ((a * 16 + r) * 4 + b, (b * 16 + r) * 4 + a) for a in range(4) for r in range(16) for b in range(4)
]


SPREAD = [
    ((a * 16 + r) * 4 + (2 * a - b + 2) % 4, (b * 16 + r) * 4 + a)
    for a in range(4) for r in range(16) for b in range(4)
]


def gather_right(own):
    pp = lax.ppermute
    z = pp(own, "zl", ring(2, 1))
    up, down, far = [pp(own, "y", ring(4, k)) for k in (1, 3, 2)]
    zdown = pp(z, "y", ring(4, 3))
    zup, zfar = pp(up, "zl", ring(2, 1)), pp(far, "zl", ring(2, 1))
    mine = [own, z, up, down, far, zup, zdown, zfar]
    return mine + [pp(m, "c", ring(2, 1)) for m in mine]


def gather_bias_z(own):
    col = jnp.stack([own] + [lax.ppermute(own, "zh", ring(4, k)) for k in (1, 2, 3)])
    return jnp.broadcast_to(col[None], (8,) + col.shape)


def body(stack, emb, entry, final, qkg, offset, out_proj, filt):
    pp = lax.ppermute
    zh, zl = lax.axis_index("zh"), lax.axis_index("zl")
    y, c, x = lax.axis_index("y"), lax.axis_index("c"), lax.axis_index("x")
    normed = standardise_features(stack).astype(BF)
    proj = jnp.einsum("sjc,cx->jxs", normed, entry, preferred_element_type=F32).astype(BF)
    left = proj[:, :PF].reshape(BLK, MSA)
    right = proj[:, PF:].transpose(1, 0, 2)
    right = jnp.concatenate([right[:, :8].reshape(8 * PF, MSA), right[:, 8:].reshape(4 * PF, MSA)], axis=0)
    row0 = (zh * 16 + zl * 8 + y * 2 + c) * ROWS
    prepared = (
        final.reshape(PF, PF, CH).transpose(1, 0, 2),
        jnp.pad(offset.T, ((0, 4), (0, 0))),
        jnp.stack([zl, y, c, zh, x, row0]).astype(jnp.int32),
    )
    right, w, off, pos = lax.optimization_barrier((pp(right, ALL, SPREAD), *prepared))
    mid, norm, bias = opm(pos, left, gather_right(right), w, emb, off)

    prev, nxt, far = [pp(norm, "x", ring(4, k)) for k in (1, 3, 2)]
    col = gather_bias_z(pp(bias, ALL, SWAP))
    prev, nxt, far, col = lax.optimization_barrier((prev, nxt, far, col))
    q, gate, kv = project(norm, prev, nxt, far, qkg)
    pay0 = lax.all_to_all(col, ("zl", "y"), 0, 0, tiled=True)
    q, gate, kv, pay0 = lax.optimization_barrier((q, gate, kv, pay0))
    pay1 = pp(pay0, "c", ring(2, 1))
    update = attend(pos, filt, q, gate, kv, pay0, pay1, out_proj)
    return mid, update


def solution(mesh):
    fine = jax.sharding.Mesh(mesh.devices.reshape(4, 2, 4, 2, 4), ALL)
    dap = ("zh", "zl", "y", "c")
    in_specs = (P(None, dap, None), P(dap, "x", None), P(), P(), P(), P(), P(), P())
    out_specs = (P(dap, "x", None), P(dap, "x", None))
    return jax.shard_map(body, mesh=fine, in_specs=in_specs, out_specs=out_specs, check_vma=False)
```

```python
import jax
import jax.numpy as jnp
from jax import lax
from jax.experimental import pallas as pl
from jax.experimental.pallas import tpu as pltpu
from jax.sharding import PartitionSpec as P

BF = jnp.bfloat16
F32 = jnp.float32
NT = (((1,), (1,)), ((), ()))
NN = (((1,), (0,)), ((), ()))

ROWS, COLS, CH, HEADS, HD = 12, 192, 128, 4, 32
MSA, MSA_CH, PF = 256, 256, 32
BLK = ROWS * PF
LANES = 128
HALF = COLS - LANES
PAY = HEADS * ROWS
LOG2E = 1.4426950408889634
TILE = 128


def ring(n, k):
    return [(i, (i + k) % n) for i in range(n)]


def dot(a, b, dims):
    return lax.dot_general(a, b, dims, preferred_element_type=F32)


VMEM = pl.BlockSpec(memory_space=pltpu.VMEM)
SMEM = pl.BlockSpec(memory_space=pltpu.SMEM)
ANY = pl.BlockSpec(memory_space=pl.ANY)
PARAMS = pltpu.CompilerParams(vmem_limit_bytes=56 * 1024 * 1024)


def msa_kernel(x_ref, w_ref, left_ref, right_ref, near, tail):
    w = w_ref[...]
    ones = jnp.ones((MSA_CH, LANES), BF)
    for j in range(ROWS):
        mean = dot(x_ref[j], ones, NN) * (1.0 / MSA_CH)
        cen = x_ref[j].astype(F32) - jnp.concatenate([mean, mean], axis=1)
        var = jnp.mean(cen * cen, axis=-1, keepdims=True)
        nrm = (cen * lax.rsqrt(var + 1e-05)).astype(BF)
        proj = dot(w, nrm, NT)
        left_ref[j * PF : (j + 1) * PF, :] = proj[:PF].astype(BF)
        if j < 8:
            near[:, j, :] = proj[PF:]
        else:
            tail[:, j - 8, :] = proj[PF:]
    right_ref[: 8 * PF, :] = near[...].reshape(8 * PF, MSA).astype(BF)
    t = tail[...].reshape(PF // 2, 2, 8, MSA)
    both = jnp.concatenate([t[:, 0, :4], t[:, 1, :4]], axis=1)
    right_ref[8 * PF :, :] = both.reshape(4 * PF, MSA).astype(BF)


def msa_project(x, w):
    return pl.pallas_call(
        msa_kernel,
        out_shape=(jax.ShapeDtypeStruct((BLK, MSA), BF), jax.ShapeDtypeStruct((BLK, MSA), BF)),
        in_specs=[VMEM, VMEM],
        out_specs=[VMEM, VMEM],
        scratch_shapes=[pltpu.VMEM((PF, 8, MSA), F32), pltpu.VMEM((PF, 8, MSA), F32)],
        compiler_params=PARAMS,
        cost_estimate=pl.CostEstimate(flops=10**8, bytes_accessed=2 * 10**6, transcendentals=10**4),
        name="msa",
    )(x, w)


PIECES = [
    (z, y, c) for c in range(2) for (z, y) in ((0, 0), (1, 0), (0, 1), (0, 3), (0, 2), (1, 1), (1, 3), (1, 2))
]


def by_channel(res, lhs, t):
    low = lax.broadcasted_iota(jnp.int32, (PF // 2, 8, LANES), 1) < 4
    for q in range(3):
        part = res[:, q * LANES : (q + 1) * LANES]
        tiles = []
        for k in range(2):
            a, b = [], []
            for c in range(2):
                base = (2 * k + c) * BLK
                a.append(part[base : base + 8 * PF].reshape(PF, 8, LANES))
                b.append(part[base + 8 * PF : base + BLK].reshape(PF // 2, 8, LANES))
            even = jnp.where(low, b[0], jnp.roll(b[1], 4, axis=1))
            odd = jnp.where(low, jnp.roll(b[0], 4, axis=1), b[1])
            tiles.append((a[0], a[1], (even, odd)))
        rows = q * COLS + t * 4 * ROWS
        for ch in range(PF):
            six = []
            for a0, a1, eo in tiles:
                six += [a0[ch], a1[ch], eo[ch % 2][ch // 2]]
            lhs[rows : rows + 4 * ROWS, ch * LANES : (ch + 1) * LANES] = jnp.concatenate(six, axis=0).astype(BF)


def natural(acc):
    n = acc.shape[1]
    p = acc.reshape(8, 3, 8, n)
    low = lax.broadcasted_iota(jnp.int32, (8, 8, n), 1) < 4
    r = jnp.roll(p[:, 1], 4, axis=1)
    mid = jnp.where(low, p[:, 2], r)
    last = jnp.where(low, r, p[:, 2])
    return jnp.concatenate([p[:, 0:1], mid[:, None], last[:, None]], axis=1).reshape(COLS, n)


def opm_kernel(pos_ref, lt_ref, *refs):
    pieces = refs[: len(PIECES)]
    (w_ref, emb_ref, off_ref, mid_ref, norm_ref, bias_ref) = refs[len(PIECES) : len(PIECES) + 6]
    (right, lhs, wblk, brow, sems) = refs[len(PIECES) + 6 :]
    zl, y, c = pos_ref[0], pos_ref[1], pos_ref[2]
    copies = []
    for n, (dz, dy, dc) in enumerate(PIECES):
        src_z = lax.rem(zl + dz, 2)
        src_y = lax.rem(y + 4 - dy, 4)
        src_c = lax.rem(c + dc, 2)
        start = (src_z * 8 + src_y * 2 + src_c) * BLK
        cp = pltpu.make_async_copy(
            pieces[n], right.at[pl.ds(pl.multiple_of(start, 128), BLK)], sems.at[n]
        )
        cp.start()
        copies.append(cp)

    def build(ch, carry):
        base = pl.multiple_of(ch * LANES, LANES)
        wy = w_ref[ch]
        zero = jnp.zeros((PF, CH), BF)
        for r in range(4):
            for t in range(4):
                wblk[pl.ds(base + r * PF, PF), t * CH : (t + 1) * CH] = wy if r == t else zero
        return carry

    lax.fori_loop(0, PF, build, 0)
    for cp in copies:
        cp.wait()

    for t in range(4):
        by_channel(dot(right[t * 4 * BLK : (t + 1) * 4 * BLK, :], lt_ref[...], NT), lhs, t)
    w = off_ref[...]
    w_hi = w.astype(BF)
    rest = w - w_hi.astype(F32)
    w_mid = rest.astype(BF)
    w_lo = (rest - w_mid.astype(F32)).astype(BF)
    w3 = jnp.concatenate([w_hi, w_mid, w_lo], axis=0)
    acc = dot(lhs[...], wblk[...], NN)
    for q in range(3):
        update = natural(acc[q * COLS : (q + 1) * COLS]) * (1.0 / MSA)
        for r in range(4):
            i = 4 * q + r
            mid = (emb_ref[i].astype(F32) + update[:, r * CH : (r + 1) * CH]).astype(BF)
            mid_ref[i] = mid
            wide = mid.astype(F32)
            cen = wide - jnp.mean(wide, axis=-1, keepdims=True)
            var = jnp.mean(cen * cen, axis=-1, keepdims=True)
            nrm = (cen * lax.rsqrt(var + 1e-05)).astype(BF)
            norm_ref[i] = nrm
            parts = dot(w3, nrm, NT)
            brow[i] = parts[0:8] + parts[8:16] + parts[16:24]
    for h in range(HEADS):
        b = brow[:, h, :]
        done = []
        tops = []
        for g in range(3):
            part = b[:, g * HALF : (g + 1) * HALF]
            top = jnp.max(part, axis=-1, keepdims=True).astype(BF).astype(F32)
            done.append(part - top)
            tops.append(top)
        lane = lax.broadcasted_iota(jnp.int32, (ROWS, HALF), 1)
        tail = jnp.where(lane == 0, tops[0], jnp.where(lane == 1, tops[1], tops[2]))
        bias_ref[h * ROWS : (h + 1) * ROWS, :] = jnp.concatenate(done + [tail], axis=1).astype(BF)


def opm(pos, left, pieces, w, emb, off):
    return pl.pallas_call(
        opm_kernel,
        out_shape=(
            jax.ShapeDtypeStruct((ROWS, COLS, CH), BF),
            jax.ShapeDtypeStruct((ROWS, COLS, CH), BF),
            jax.ShapeDtypeStruct((PAY, 2 * LANES), BF),
        ),
        in_specs=[SMEM, VMEM] + [ANY] * len(PIECES) + [VMEM] * 3,
        out_specs=[VMEM] * 3,
        scratch_shapes=[
            pltpu.VMEM((16 * BLK, MSA), BF),
            pltpu.VMEM((3 * COLS, PF * LANES), BF),
            pltpu.VMEM((PF * LANES, 4 * CH), BF),
            pltpu.VMEM((ROWS, 8, COLS), F32),
            pltpu.SemaphoreType.DMA((len(PIECES),)),
        ],
        compiler_params=PARAMS,
        cost_estimate=pl.CostEstimate(flops=6 * 10**9, bytes_accessed=10**7, transcendentals=0),
        name="opm",
    )(pos, left, *pieces, w, emb, off)


AT_ROWS = 3
PR_ROWS = 4


def project_kernel(own_ref, prev_ref, next_ref, far_ref, qkg_ref, q_ref, gate_ref, kv_ref):
    for r in range(PR_ROWS):
        own = own_ref[r]
        four = (own, prev_ref[r], next_ref[r], far_ref[r])
        keys_in = jnp.concatenate([f[:LANES] for f in four] + [f[LANES:] for f in four], axis=0)
        q_ref[r] = (dot(own, qkg_ref[:, :CH], NN) * (HD ** (-0.5) * LOG2E)).astype(BF)
        gate_ref[r] = jax.nn.sigmoid(dot(own, qkg_ref[:, 3 * CH :], NN))
        kv_ref[r] = dot(keys_in, qkg_ref[:, CH : 3 * CH], NN).astype(BF)


def project(own, prev, nxt, far, qkg):
    row = pl.BlockSpec((PR_ROWS, COLS, CH), lambda i: (i, 0, 0))
    return pl.pallas_call(
        project_kernel,
        grid=(ROWS // PR_ROWS,),
        out_shape=(
            jax.ShapeDtypeStruct((ROWS, COLS, CH), BF),
            jax.ShapeDtypeStruct((ROWS, COLS, CH), F32),
            jax.ShapeDtypeStruct((ROWS, 4 * COLS, 2 * CH), BF),
        ),
        in_specs=[row] * 4 + [VMEM],
        out_specs=[row, row, pl.BlockSpec((PR_ROWS, 4 * COLS, 2 * CH), lambda i: (i, 0, 0))],
        compiler_params=PARAMS,
        cost_estimate=pl.CostEstimate(flops=10**10, bytes_accessed=2 * 10**7, transcendentals=10**5),
        name="project",
    )(own, prev, nxt, far, qkg)


def attend_kernel(
    pos_ref, filt_ref, q_ref, gate_ref, kv_ref, pay0_ref, pay1_ref, wo_ref, out_ref, bias,
):
    i = pl.program_id(0)
    c, zh, x = pos_ref[2], pos_ref[3], pos_ref[4]

    @pl.when(i == 0)
    def _():
        first_lane = lax.broadcasted_iota(jnp.int32, (PAY, LANES), 1) < HALF

        def place(pair, carry):
            row0 = pl.multiple_of(pair * 2 * ROWS, 8)
            tails = []
            for rel, shift in enumerate((0, 3, 1, 2)):
                at = lax.rem(zh + 8 - x - shift, 4)
                p0 = pay0_ref[pair, at].astype(F32) * LOG2E
                p1 = pay1_ref[pair, at].astype(F32) * LOG2E
                heads = []
                for p in (jnp.where(c == 0, p0, p1), jnp.where(c == 0, p1, p0)):
                    m = COLS
                    heads.append(
                        p[:, :LANES] + jnp.where(first_lane, p[:, m : m + 1], p[:, m + 1 : m + 2])
                    )
                    tails.append(p[:, LANES:COLS] + p[:, m + 2 : m + 3])
                for h in range(HEADS):
                    cut = slice(h * ROWS, (h + 1) * ROWS)
                    bias[h, pl.ds(row0, 2 * ROWS), rel * LANES : (rel + 1) * LANES] = jnp.concatenate(
                        [heads[0][cut], heads[1][cut]], axis=0
                    )
            for half in range(2):
                t = tails[4 * half : 4 * half + 4]
                both = [jnp.concatenate([t[0], t[2]], axis=1), jnp.concatenate([t[1], t[3]], axis=1)]
                lane = (4 + half) * LANES
                for h in range(HEADS):
                    cut = slice(h * ROWS, (h + 1) * ROWS)
                    bias[h, pl.ds(row0, 2 * ROWS), lane : lane + LANES] = jnp.concatenate(
                        [both[0][cut], both[1][cut]], axis=0
                    )
            return carry

        lax.fori_loop(0, 8, place, 0)

    run = lax.broadcasted_iota(jnp.int32, (1, 4 * COLS), 1) // HALF
    lane_head = lax.broadcasted_iota(jnp.int32, (COLS, CH), 1) // HD
    for r in range(AT_ROWS):
        q, k = q_ref[r], kv_ref[r, :, :CH]
        v1 = jnp.concatenate([kv_ref[r, :, CH:], jnp.ones((4 * COLS, CH), BF)], axis=1)
        row_tile = (pos_ref[5] + i * AT_ROWS + r) // TILE
        pen = jnp.zeros((1, 4 * COLS), F32)
        for rel, shift in enumerate((0, 3, 1, 2)):
            col = lax.rem(x + shift, 4) * COLS
            for slot, start in ((2 * rel, 0), (2 * rel + 1, HALF), (8 + rel, LANES)):
                keep = filt_ref[row_tile, (col + start) // TILE]
                pen = jnp.where(run == slot, (keep.astype(F32) - 1.0) * 1000000000.0, pen)
        att = jnp.zeros((COLS, CH), F32)
        for h in range(HEADS):
            mine = lane_head == h
            qh = jnp.where(mine, q, jnp.zeros_like(q))
            s = dot(qh, k, NT) + bias[h] + pen
            p = jnp.exp2(s - jnp.max(s, axis=-1, keepdims=True)).astype(BF)
            o = dot(p, v1, NN)
            att = jnp.where(mine, o[:, :CH] / o[:, CH:], att)
        gated = (gate_ref[r] * att).astype(BF)
        out_ref[r] = dot(gated, wo_ref[...], NN).astype(BF)


def attend(pos, filt, q, gate, kv, pay0, pay1, wo):
    row = pl.BlockSpec((AT_ROWS, COLS, CH), lambda i: (i, 0, 0))
    keys = pl.BlockSpec((AT_ROWS, 4 * COLS, 2 * CH), lambda i: (i, 0, 0))
    return pl.pallas_call(
        attend_kernel,
        grid=(ROWS // AT_ROWS,),
        out_shape=jax.ShapeDtypeStruct((ROWS, COLS, CH), BF),
        in_specs=[SMEM, SMEM, row, row, keys] + [VMEM] * 3,
        out_specs=row,
        scratch_shapes=[pltpu.VMEM((HEADS, COLS, 4 * COLS), F32)],
        compiler_params=PARAMS,
        cost_estimate=pl.CostEstimate(flops=8 * 10**9, bytes_accessed=10**7, transcendentals=7 * 10**6),
        name="attend",
    )(pos, filt, q, gate, kv, pay0, pay1, wo)


ALL = ("zh", "zl", "y", "c", "x")
SWAP = [
    ((a * 16 + r) * 4 + b, (b * 16 + r) * 4 + a) for a in range(4) for r in range(16) for b in range(4)
]


SPREAD = [
    ((a * 16 + r) * 4 + (2 * a - b + 2) % 4, (b * 16 + r) * 4 + a)
    for a in range(4) for r in range(16) for b in range(4)
]


def gather_right(own):
    pp = lax.ppermute
    z = pp(own, "zl", ring(2, 1))
    up, down, far = [pp(own, "y", ring(4, k)) for k in (1, 3, 2)]
    zdown = pp(z, "y", ring(4, 3))
    zup, zfar = pp(up, "zl", ring(2, 1)), pp(far, "zl", ring(2, 1))
    mine = [own, z, up, down, far, zup, zdown, zfar]
    return mine + [pp(m, "c", ring(2, 1)) for m in mine]


def gather_bias_z(own):
    col = jnp.stack([own] + [lax.ppermute(own, "zh", ring(4, k)) for k in (1, 2, 3)])
    return jnp.broadcast_to(col[None], (8,) + col.shape)


def body(stack, emb, entry, final, qkg, offset, out_proj, filt):
    pp = lax.ppermute
    zh, zl = lax.axis_index("zh"), lax.axis_index("zl")
    y, c, x = lax.axis_index("y"), lax.axis_index("c"), lax.axis_index("x")
    left, right = msa_project(stack.transpose(1, 0, 2), entry.T)
    row0 = (zh * 16 + zl * 8 + y * 2 + c) * ROWS
    prepared = (
        final.reshape(PF, PF, CH).transpose(1, 0, 2),
        jnp.pad(offset.T, ((0, 4), (0, 0))),
        jnp.stack([zl, y, c, zh, x, row0]).astype(jnp.int32),
    )
    right, w, off, pos = lax.optimization_barrier((pp(right, ALL, SPREAD), *prepared))
    mid, norm, bias = opm(pos, left, gather_right(right), w, emb, off)

    prev, nxt, far = [pp(norm, "x", ring(4, k)) for k in (1, 3, 2)]
    col = gather_bias_z(pp(bias, ALL, SWAP))
    prev, nxt, far, col = lax.optimization_barrier((prev, nxt, far, col))
    q, gate, kv = project(norm, prev, nxt, far, qkg)
    pay0 = lax.all_to_all(col, ("zl", "y"), 0, 0, tiled=True)
    q, gate, kv, pay0 = lax.optimization_barrier((q, gate, kv, pay0))
    pay1 = pp(pay0, "c", ring(2, 1))
    update = attend(pos, filt, q, gate, kv, pay0, pay1, out_proj)
    return mid, update


def solution(mesh):
    fine = jax.sharding.Mesh(mesh.devices.reshape(4, 2, 4, 2, 4), ALL)
    dap = ("zh", "zl", "y", "c")
    in_specs = (P(None, dap, None), P(dap, "x", None), P(), P(), P(), P(), P(), P())
    out_specs = (P(dap, "x", None), P(dap, "x", None))
    return jax.shard_map(body, mesh=fine, in_specs=in_specs, out_specs=out_specs, check_vma=False)
```

```python
import jax
import jax.numpy as jnp
from jax import lax
from jax.experimental import pallas as pl
from jax.experimental.pallas import tpu as pltpu
from jax.sharding import PartitionSpec as P

BF = jnp.bfloat16
F32 = jnp.float32
NT = (((1,), (1,)), ((), ()))
NN = (((1,), (0,)), ((), ()))

ROWS, COLS, CH, HEADS, HD = 12, 192, 128, 4, 32
MSA, MSA_CH, PF = 256, 256, 32
BLK = ROWS * PF
LANES = 128
HALF = COLS - LANES
PAY = HEADS * ROWS
LOG2E = 1.4426950408889634
TILE = 128


def ring(n, k):
    return [(i, (i + k) % n) for i in range(n)]


def dot(a, b, dims):
    return lax.dot_general(a, b, dims, preferred_element_type=F32)


VMEM = pl.BlockSpec(memory_space=pltpu.VMEM)
SMEM = pl.BlockSpec(memory_space=pltpu.SMEM)
ANY = pl.BlockSpec(memory_space=pl.ANY)
PARAMS = pltpu.CompilerParams(vmem_limit_bytes=56 * 1024 * 1024)


def msa_kernel(x_ref, w_ref, left_ref, right_ref, near, tail):
    w = w_ref[...]
    ones = jnp.ones((MSA_CH, LANES), BF)
    for j in range(ROWS):
        mean = dot(x_ref[j], ones, NN) * (1.0 / MSA_CH)
        cen = x_ref[j].astype(F32) - jnp.concatenate([mean, mean], axis=1)
        var = jnp.mean(cen * cen, axis=-1, keepdims=True)
        nrm = (cen * lax.rsqrt(var + 1e-05)).astype(BF)
        proj = dot(w, nrm, NT)
        left_ref[j * PF : (j + 1) * PF, :] = proj[:PF].astype(BF)
        if j < 8:
            near[:, j, :] = proj[PF:]
        else:
            tail[:, j - 8, :] = proj[PF:]
    right_ref[: 8 * PF, :] = near[...].reshape(8 * PF, MSA).astype(BF)
    t = tail[...].reshape(PF // 2, 2, 8, MSA)
    both = jnp.concatenate([t[:, 0, :4], t[:, 1, :4]], axis=1)
    right_ref[8 * PF :, :] = both.reshape(4 * PF, MSA).astype(BF)


def msa_project(x, w):
    return pl.pallas_call(
        msa_kernel,
        out_shape=(jax.ShapeDtypeStruct((BLK, MSA), BF), jax.ShapeDtypeStruct((BLK, MSA), BF)),
        in_specs=[VMEM, VMEM],
        out_specs=[VMEM, VMEM],
        scratch_shapes=[pltpu.VMEM((PF, 8, MSA), F32), pltpu.VMEM((PF, 8, MSA), F32)],
        compiler_params=PARAMS,
        cost_estimate=pl.CostEstimate(flops=10**8, bytes_accessed=2 * 10**6, transcendentals=10**4),
        name="msa",
    )(x, w)


PIECES = [
    (z, y, c) for c in range(2) for (z, y) in ((0, 0), (1, 0), (0, 1), (0, 3), (0, 2), (1, 1), (1, 3), (1, 2))
]


def by_channel(res, lhs, t):
    low = lax.broadcasted_iota(jnp.int32, (PF // 2, 8, LANES), 1) < 4
    for q in range(3):
        part = res[:, q * LANES : (q + 1) * LANES]
        tiles = []
        for k in range(2):
            a, b = [], []
            for c in range(2):
                base = (2 * k + c) * BLK
                a.append(part[base : base + 8 * PF].reshape(PF, 8, LANES))
                b.append(part[base + 8 * PF : base + BLK].reshape(PF // 2, 8, LANES))
            even = jnp.where(low, b[0], jnp.roll(b[1], 4, axis=1))
            odd = jnp.where(low, jnp.roll(b[0], 4, axis=1), b[1])
            tiles.append((a[0], a[1], (even, odd)))
        rows = q * COLS + t * 4 * ROWS
        for ch in range(PF):
            six = []
            for a0, a1, eo in tiles:
                six += [a0[ch], a1[ch], eo[ch % 2][ch // 2]]
            lhs[rows : rows + 4 * ROWS, ch * LANES : (ch + 1) * LANES] = jnp.concatenate(six, axis=0).astype(BF)


def natural(acc):
    n = acc.shape[1]
    p = acc.reshape(8, 3, 8, n)
    low = lax.broadcasted_iota(jnp.int32, (8, 8, n), 1) < 4
    r = jnp.roll(p[:, 1], 4, axis=1)
    mid = jnp.where(low, p[:, 2], r)
    last = jnp.where(low, r, p[:, 2])
    return jnp.concatenate([p[:, 0:1], mid[:, None], last[:, None]], axis=1).reshape(COLS, n)


def opm_kernel(pos_ref, lt_ref, *refs):
    pieces = refs[: len(PIECES)]
    (w_ref, emb_ref, off_ref, mid_ref, norm_ref, bias_ref) = refs[len(PIECES) : len(PIECES) + 6]
    (right, lhs, wblk, brow, sems) = refs[len(PIECES) + 6 :]
    zl, y, c = pos_ref[0], pos_ref[1], pos_ref[2]
    copies = []
    for n, (dz, dy, dc) in enumerate(PIECES):
        src_z = lax.rem(zl + dz, 2)
        src_y = lax.rem(y + 4 - dy, 4)
        src_c = lax.rem(c + dc, 2)
        start = (src_z * 8 + src_y * 2 + src_c) * BLK
        cp = pltpu.make_async_copy(
            pieces[n], right.at[pl.ds(pl.multiple_of(start, 128), BLK)], sems.at[n]
        )
        cp.start()
        copies.append(cp)

    def build(ch, carry):
        base = pl.multiple_of(ch * LANES, LANES)
        wy = w_ref[ch]
        zero = jnp.zeros((PF, CH), BF)
        for r in range(4):
            for t in range(4):
                wblk[pl.ds(base + r * PF, PF), t * CH : (t + 1) * CH] = wy if r == t else zero
        return carry

    lax.fori_loop(0, PF, build, 0)
    for cp in copies:
        cp.wait()

    for t in range(4):
        by_channel(dot(right[t * 4 * BLK : (t + 1) * 4 * BLK, :], lt_ref[...], NT), lhs, t)
    w = off_ref[...]
    w_hi = w.astype(BF)
    rest = w - w_hi.astype(F32)
    w_mid = rest.astype(BF)
    w_lo = (rest - w_mid.astype(F32)).astype(BF)
    w3 = jnp.concatenate([w_hi, w_mid, w_lo], axis=0)
    acc = dot(lhs[...], wblk[...], NN)
    for q in range(3):
        update = natural(acc[q * COLS : (q + 1) * COLS]) * (1.0 / MSA)
        for r in range(4):
            i = 4 * q + r
            mid = (emb_ref[i].astype(F32) + update[:, r * CH : (r + 1) * CH]).astype(BF)
            mid_ref[i] = mid
            wide = mid.astype(F32)
            cen = wide - jnp.mean(wide, axis=-1, keepdims=True)
            var = jnp.mean(cen * cen, axis=-1, keepdims=True)
            nrm = (cen * lax.rsqrt(var + 1e-05)).astype(BF)
            norm_ref[i] = nrm
            parts = dot(w3, nrm, NT)
            brow[i] = parts[0:8] + parts[8:16] + parts[16:24]
    for h in range(HEADS):
        b = brow[:, h, :]
        done = []
        tops = []
        for g in range(3):
            part = b[:, g * HALF : (g + 1) * HALF]
            top = jnp.max(part, axis=-1, keepdims=True).astype(BF).astype(F32)
            done.append(part - top)
            tops.append(top)
        lane = lax.broadcasted_iota(jnp.int32, (ROWS, HALF), 1)
        tail = jnp.where(lane == 0, tops[0], jnp.where(lane == 1, tops[1], tops[2]))
        bias_ref[h * ROWS : (h + 1) * ROWS, :] = jnp.concatenate(done + [tail], axis=1).astype(BF)


def opm(pos, left, pieces, w, emb, off):
    return pl.pallas_call(
        opm_kernel,
        out_shape=(
            jax.ShapeDtypeStruct((ROWS, COLS, CH), BF),
            jax.ShapeDtypeStruct((ROWS, COLS, CH), BF),
            jax.ShapeDtypeStruct((PAY, 2 * LANES), BF),
        ),
        in_specs=[SMEM, VMEM] + [ANY] * len(PIECES) + [VMEM] * 3,
        out_specs=[VMEM] * 3,
        scratch_shapes=[
            pltpu.VMEM((16 * BLK, MSA), BF),
            pltpu.VMEM((3 * COLS, PF * LANES), BF),
            pltpu.VMEM((PF * LANES, 4 * CH), BF),
            pltpu.VMEM((ROWS, 8, COLS), F32),
            pltpu.SemaphoreType.DMA((len(PIECES),)),
        ],
        compiler_params=PARAMS,
        cost_estimate=pl.CostEstimate(flops=6 * 10**9, bytes_accessed=10**7, transcendentals=0),
        name="opm",
    )(pos, left, *pieces, w, emb, off)


AT_ROWS = 3
PR_ROWS = 4


def project_kernel(own_ref, prev_ref, next_ref, far_ref, qkg_ref, q_ref, gate_ref, kv_ref):
    for r in range(PR_ROWS):
        own = own_ref[r]
        four = (own, prev_ref[r], next_ref[r], far_ref[r])
        keys_in = jnp.concatenate([f[:LANES] for f in four] + [f[LANES:] for f in four], axis=0)
        q_ref[r] = (dot(own, qkg_ref[:, :CH], NN) * (HD ** (-0.5) * LOG2E)).astype(BF)
        gate_ref[r] = jax.nn.sigmoid(dot(own, qkg_ref[:, 3 * CH :], NN))
        kv_ref[r] = dot(keys_in, qkg_ref[:, CH : 3 * CH], NN).astype(BF)


def project(own, prev, nxt, far, qkg):
    row = pl.BlockSpec((PR_ROWS, COLS, CH), lambda i: (i, 0, 0))
    return pl.pallas_call(
        project_kernel,
        grid=(ROWS // PR_ROWS,),
        out_shape=(
            jax.ShapeDtypeStruct((ROWS, COLS, CH), BF),
            jax.ShapeDtypeStruct((ROWS, COLS, CH), F32),
            jax.ShapeDtypeStruct((ROWS, 4 * COLS, 2 * CH), BF),
        ),
        in_specs=[row] * 4 + [VMEM],
        out_specs=[row, row, pl.BlockSpec((PR_ROWS, 4 * COLS, 2 * CH), lambda i: (i, 0, 0))],
        compiler_params=PARAMS,
        cost_estimate=pl.CostEstimate(flops=10**10, bytes_accessed=2 * 10**7, transcendentals=10**5),
        name="project",
    )(own, prev, nxt, far, qkg)


def attend_kernel(
    pos_ref, filt_ref, q_ref, gate_ref, kv_ref, pay0_ref, pay1_ref, wo_ref, out_ref, bias,
):
    i = pl.program_id(0)
    c, zh, x = pos_ref[2], pos_ref[3], pos_ref[4]

    @pl.when(i == 0)
    def _():
        first_lane = lax.broadcasted_iota(jnp.int32, (PAY, LANES), 1) < HALF

        def place(pair, carry):
            row0 = pl.multiple_of(pair * 2 * ROWS, 8)
            tails = []
            for rel, shift in enumerate((0, 3, 1, 2)):
                at = lax.rem(zh + 8 - x - shift, 4)
                p0 = pay0_ref[pair, at].astype(F32) * LOG2E
                p1 = pay1_ref[pair, at].astype(F32) * LOG2E
                heads = []
                for p in (jnp.where(c == 0, p0, p1), jnp.where(c == 0, p1, p0)):
                    m = COLS
                    heads.append(
                        p[:, :LANES] + jnp.where(first_lane, p[:, m : m + 1], p[:, m + 1 : m + 2])
                    )
                    tails.append(p[:, LANES:COLS] + p[:, m + 2 : m + 3])
                for h in range(HEADS):
                    cut = slice(h * ROWS, (h + 1) * ROWS)
                    bias[h, pl.ds(row0, 2 * ROWS), rel * LANES : (rel + 1) * LANES] = jnp.concatenate(
                        [heads[0][cut], heads[1][cut]], axis=0
                    )
            for half in range(2):
                t = tails[4 * half : 4 * half + 4]
                both = [jnp.concatenate([t[0], t[2]], axis=1), jnp.concatenate([t[1], t[3]], axis=1)]
                lane = (4 + half) * LANES
                for h in range(HEADS):
                    cut = slice(h * ROWS, (h + 1) * ROWS)
                    bias[h, pl.ds(row0, 2 * ROWS), lane : lane + LANES] = jnp.concatenate(
                        [both[0][cut], both[1][cut]], axis=0
                    )
            return carry

        lax.fori_loop(0, 8, place, 0, unroll=2)

    run = lax.broadcasted_iota(jnp.int32, (1, 4 * COLS), 1) // HALF
    lane_head = lax.broadcasted_iota(jnp.int32, (COLS, CH), 1) // HD
    for r in range(AT_ROWS):
        q, k = q_ref[r], kv_ref[r, :, :CH]
        v1 = jnp.concatenate([kv_ref[r, :, CH:], jnp.ones((4 * COLS, CH), BF)], axis=1)
        row_tile = (pos_ref[5] + i * AT_ROWS + r) // TILE
        pen = jnp.zeros((1, 4 * COLS), F32)
        for rel, shift in enumerate((0, 3, 1, 2)):
            col = lax.rem(x + shift, 4) * COLS
            for slot, start in ((2 * rel, 0), (2 * rel + 1, HALF), (8 + rel, LANES)):
                keep = filt_ref[row_tile, (col + start) // TILE]
                pen = jnp.where(run == slot, (keep.astype(F32) - 1.0) * 1000000000.0, pen)
        att = jnp.zeros((COLS, CH), F32)
        for h in range(HEADS):
            mine = lane_head == h
            qh = jnp.where(mine, q, jnp.zeros_like(q))
            s = dot(qh, k, NT) + bias[h] + pen
            p = jnp.exp2((s - jnp.max(s, axis=-1, keepdims=True)).astype(BF))
            o = dot(p, v1, NN)
            att = jnp.where(mine, o[:, :CH] / o[:, CH:], att)
        gated = (gate_ref[r] * att).astype(BF)
        out_ref[r] = dot(gated, wo_ref[...], NN).astype(BF)


def attend(pos, filt, q, gate, kv, pay0, pay1, wo):
    row = pl.BlockSpec((AT_ROWS, COLS, CH), lambda i: (i, 0, 0))
    keys = pl.BlockSpec((AT_ROWS, 4 * COLS, 2 * CH), lambda i: (i, 0, 0))
    return pl.pallas_call(
        attend_kernel,
        grid=(ROWS // AT_ROWS,),
        out_shape=jax.ShapeDtypeStruct((ROWS, COLS, CH), BF),
        in_specs=[SMEM, SMEM, row, row, keys] + [VMEM] * 3,
        out_specs=row,
        scratch_shapes=[pltpu.VMEM((HEADS, COLS, 4 * COLS), F32)],
        compiler_params=PARAMS,
        cost_estimate=pl.CostEstimate(flops=8 * 10**9, bytes_accessed=10**7, transcendentals=7 * 10**6),
        name="attend",
    )(pos, filt, q, gate, kv, pay0, pay1, wo)


ALL = ("zh", "zl", "y", "c", "x")
SWAP = [
    ((a * 16 + r) * 4 + b, (b * 16 + r) * 4 + a) for a in range(4) for r in range(16) for b in range(4)
]


SPREAD = [
    ((a * 16 + r) * 4 + (2 * a - b + 2) % 4, (b * 16 + r) * 4 + a)
    for a in range(4) for r in range(16) for b in range(4)
]


def gather_right(own):
    pp = lax.ppermute
    z = pp(own, "zl", ring(2, 1))
    up, down, far = [pp(own, "y", ring(4, k)) for k in (1, 3, 2)]
    zdown = pp(z, "y", ring(4, 3))
    zup, zfar = pp(up, "zl", ring(2, 1)), pp(far, "zl", ring(2, 1))
    mine = [own, z, up, down, far, zup, zdown, zfar]
    return mine + [pp(m, "c", ring(2, 1)) for m in mine]


def gather_bias_z(own):
    col = jnp.stack([own] + [lax.ppermute(own, "zh", ring(4, k)) for k in (1, 2, 3)])
    return jnp.broadcast_to(col[None], (8,) + col.shape)


def body(stack, emb, entry, final, qkg, offset, out_proj, filt):
    pp = lax.ppermute
    zh, zl = lax.axis_index("zh"), lax.axis_index("zl")
    y, c, x = lax.axis_index("y"), lax.axis_index("c"), lax.axis_index("x")
    left, right = msa_project(stack.transpose(1, 0, 2), entry.T)
    row0 = (zh * 16 + zl * 8 + y * 2 + c) * ROWS
    prepared = (
        final.reshape(PF, PF, CH).transpose(1, 0, 2),
        jnp.pad(offset.T, ((0, 4), (0, 0))),
        jnp.stack([zl, y, c, zh, x, row0]).astype(jnp.int32),
    )
    right, w, off, pos = lax.optimization_barrier((pp(right, ALL, SPREAD), *prepared))
    mid, norm, bias = opm(pos, left, gather_right(right), w, emb, off)

    prev, nxt, far = [pp(norm, "x", ring(4, k)) for k in (1, 3, 2)]
    col = gather_bias_z(pp(bias, ALL, SWAP))
    prev, nxt, far, col = lax.optimization_barrier((prev, nxt, far, col))
    q, gate, kv = project(norm, prev, nxt, far, qkg)
    pay0 = lax.all_to_all(col, ("zl", "y"), 0, 0, tiled=True)
    q, gate, kv, pay0 = lax.optimization_barrier((q, gate, kv, pay0))
    pay1 = pp(pay0, "c", ring(2, 1))
    update = attend(pos, filt, q, gate, kv, pay0, pay1, out_proj)
    return mid, update


def solution(mesh):
    fine = jax.sharding.Mesh(mesh.devices.reshape(4, 2, 4, 2, 4), ALL)
    dap = ("zh", "zl", "y", "c")
    in_specs = (P(None, dap, None), P(dap, "x", None), P(), P(), P(), P(), P(), P())
    out_specs = (P(dap, "x", None), P(dap, "x", None))
    return jax.shard_map(body, mesh=fine, in_specs=in_specs, out_specs=out_specs, check_vma=False)
```

```python
import jax
import jax.numpy as jnp
from jax import lax
from jax.experimental import pallas as pl
from jax.experimental.pallas import tpu as pltpu
from jax.sharding import PartitionSpec as P

BF = jnp.bfloat16
F32 = jnp.float32
NT = (((1,), (1,)), ((), ()))
NN = (((1,), (0,)), ((), ()))

ROWS, COLS, CH, HEADS, HD = 12, 192, 128, 4, 32
MSA, MSA_CH, PF = 256, 256, 32
BLK = ROWS * PF
LANES = 128
HALF = COLS - LANES
PAY = HEADS * ROWS
LOG2E = 1.4426950408889634
TILE = 128


def ring(n, k):
    return [(i, (i + k) % n) for i in range(n)]


def dot(a, b, dims):
    return lax.dot_general(a, b, dims, preferred_element_type=F32)


VMEM = pl.BlockSpec(memory_space=pltpu.VMEM)
SMEM = pl.BlockSpec(memory_space=pltpu.SMEM)
ANY = pl.BlockSpec(memory_space=pl.ANY)
PARAMS = pltpu.CompilerParams(vmem_limit_bytes=56 * 1024 * 1024)


def msa_kernel(x_ref, w_ref, left_ref, right_ref, near, tail):
    w = w_ref[...]
    ones = jnp.ones((MSA_CH, LANES), BF)
    for j in range(ROWS):
        mean = dot(x_ref[j], ones, NN) * (1.0 / MSA_CH)
        cen = x_ref[j].astype(F32) - jnp.concatenate([mean, mean], axis=1)
        var = jnp.mean(cen * cen, axis=-1, keepdims=True)
        nrm = (cen * lax.rsqrt(var + 1e-05)).astype(BF)
        proj = dot(w, nrm, NT)
        left_ref[j * PF : (j + 1) * PF, :] = proj[:PF].astype(BF)
        if j < 8:
            near[:, j, :] = proj[PF:]
        else:
            tail[:, j - 8, :] = proj[PF:]
    right_ref[: 8 * PF, :] = near[...].reshape(8 * PF, MSA).astype(BF)
    t = tail[...].reshape(PF // 2, 2, 8, MSA)
    both = jnp.concatenate([t[:, 0, :4], t[:, 1, :4]], axis=1)
    right_ref[8 * PF :, :] = both.reshape(4 * PF, MSA).astype(BF)


def msa_project(x, w):
    return pl.pallas_call(
        msa_kernel,
        out_shape=(jax.ShapeDtypeStruct((BLK, MSA), BF), jax.ShapeDtypeStruct((BLK, MSA), BF)),
        in_specs=[VMEM, VMEM],
        out_specs=[VMEM, VMEM],
        scratch_shapes=[pltpu.VMEM((PF, 8, MSA), F32), pltpu.VMEM((PF, 8, MSA), F32)],
        compiler_params=PARAMS,
        cost_estimate=pl.CostEstimate(flops=10**8, bytes_accessed=2 * 10**6, transcendentals=10**4),
        name="msa",
    )(x, w)


PIECES = [
    (z, y, c) for c in range(2) for (z, y) in ((0, 0), (1, 0), (0, 1), (0, 3), (0, 2), (1, 1), (1, 3), (1, 2))
]


def by_channel(res, lhs, t):
    low = lax.broadcasted_iota(jnp.int32, (PF // 2, 8, LANES), 1) < 4
    for q in range(3):
        part = res[:, q * LANES : (q + 1) * LANES]
        tiles = []
        for k in range(2):
            a, b = [], []
            for c in range(2):
                base = (2 * k + c) * BLK
                a.append(part[base : base + 8 * PF].reshape(PF, 8, LANES))
                b.append(part[base + 8 * PF : base + BLK].reshape(PF // 2, 8, LANES))
            even = jnp.where(low, b[0], jnp.roll(b[1], 4, axis=1))
            odd = jnp.where(low, jnp.roll(b[0], 4, axis=1), b[1])
            tiles.append((a[0], a[1], (even, odd)))
        rows = q * COLS + t * 4 * ROWS
        for ch in range(PF):
            six = []
            for a0, a1, eo in tiles:
                six += [a0[ch], a1[ch], eo[ch % 2][ch // 2]]
            lhs[rows : rows + 4 * ROWS, ch * LANES : (ch + 1) * LANES] = jnp.concatenate(six, axis=0).astype(BF)


def natural(acc):
    n = acc.shape[1]
    p = acc.reshape(8, 3, 8, n)
    low = lax.broadcasted_iota(jnp.int32, (8, 8, n), 1) < 4
    r = jnp.roll(p[:, 1], 4, axis=1)
    mid = jnp.where(low, p[:, 2], r)
    last = jnp.where(low, r, p[:, 2])
    return jnp.concatenate([p[:, 0:1], mid[:, None], last[:, None]], axis=1).reshape(COLS, n)


def opm_kernel(pos_ref, lt_ref, *refs):
    pieces = refs[: len(PIECES)]
    (w_ref, emb_ref, off_ref, mid_ref, norm_ref, bias_ref) = refs[len(PIECES) : len(PIECES) + 6]
    (right, lhs, wblk, brow, sems) = refs[len(PIECES) + 6 :]
    zl, y, c = pos_ref[0], pos_ref[1], pos_ref[2]
    copies = []
    for n, (dz, dy, dc) in enumerate(PIECES):
        src_z = lax.rem(zl + dz, 2)
        src_y = lax.rem(y + 4 - dy, 4)
        src_c = lax.rem(c + dc, 2)
        start = (src_z * 8 + src_y * 2 + src_c) * BLK
        cp = pltpu.make_async_copy(
            pieces[n], right.at[pl.ds(pl.multiple_of(start, 128), BLK)], sems.at[n]
        )
        cp.start()
        copies.append(cp)

    def build(ch, carry):
        base = pl.multiple_of(ch * LANES, LANES)
        wy = w_ref[ch]
        zero = jnp.zeros((PF, CH), BF)
        for r in range(4):
            for t in range(4):
                wblk[pl.ds(base + r * PF, PF), t * CH : (t + 1) * CH] = wy if r == t else zero
        return carry

    lax.fori_loop(0, PF, build, 0)
    for cp in copies:
        cp.wait()

    for t in range(4):
        by_channel(dot(right[t * 4 * BLK : (t + 1) * 4 * BLK, :], lt_ref[...], NT), lhs, t)
    w = off_ref[...]
    w_hi = w.astype(BF)
    rest = w - w_hi.astype(F32)
    w_mid = rest.astype(BF)
    w_lo = (rest - w_mid.astype(F32)).astype(BF)
    w3 = jnp.concatenate([w_hi, w_mid, w_lo], axis=0)
    acc = dot(lhs[...], wblk[...], NN)
    for q in range(3):
        update = natural(acc[q * COLS : (q + 1) * COLS]) * (1.0 / MSA)
        for r in range(4):
            i = 4 * q + r
            mid = (emb_ref[i].astype(F32) + update[:, r * CH : (r + 1) * CH]).astype(BF)
            mid_ref[i] = mid
            wide = mid.astype(F32)
            cen = wide - jnp.mean(wide, axis=-1, keepdims=True)
            var = jnp.mean(cen * cen, axis=-1, keepdims=True)
            nrm = (cen * lax.rsqrt(var + 1e-05)).astype(BF)
            norm_ref[i] = nrm
            parts = dot(w3, nrm, NT)
            brow[i] = parts[0:8] + parts[8:16] + parts[16:24]
    for h in range(HEADS):
        b = brow[:, h, :]
        done = []
        tops = []
        for g in range(3):
            part = b[:, g * HALF : (g + 1) * HALF]
            top = jnp.max(part, axis=-1, keepdims=True).astype(BF).astype(F32)
            done.append(part - top)
            tops.append(top)
        lane = lax.broadcasted_iota(jnp.int32, (ROWS, HALF), 1)
        tail = jnp.where(lane == 0, tops[0], jnp.where(lane == 1, tops[1], tops[2]))
        bias_ref[h * ROWS : (h + 1) * ROWS, :] = jnp.concatenate(done + [tail], axis=1).astype(BF)


def opm(pos, left, pieces, w, emb, off):
    return pl.pallas_call(
        opm_kernel,
        out_shape=(
            jax.ShapeDtypeStruct((ROWS, COLS, CH), BF),
            jax.ShapeDtypeStruct((ROWS, COLS, CH), BF),
            jax.ShapeDtypeStruct((PAY, 2 * LANES), BF),
        ),
        in_specs=[SMEM, VMEM] + [ANY] * len(PIECES) + [VMEM] * 3,
        out_specs=[VMEM] * 3,
        scratch_shapes=[
            pltpu.VMEM((16 * BLK, MSA), BF),
            pltpu.VMEM((3 * COLS, PF * LANES), BF),
            pltpu.VMEM((PF * LANES, 4 * CH), BF),
            pltpu.VMEM((ROWS, 8, COLS), F32),
            pltpu.SemaphoreType.DMA((len(PIECES),)),
        ],
        compiler_params=PARAMS,
        cost_estimate=pl.CostEstimate(flops=6 * 10**9, bytes_accessed=10**7, transcendentals=0),
        name="opm",
    )(pos, left, *pieces, w, emb, off)


AT_ROWS = 3
PR_ROWS = 4


def project_kernel(own_ref, prev_ref, next_ref, far_ref, qkg_ref, q_ref, gate_ref, kv_ref):
    for r in range(PR_ROWS):
        own = own_ref[r]
        four = (own, prev_ref[r], next_ref[r], far_ref[r])
        keys_in = jnp.concatenate([f[:LANES] for f in four] + [f[LANES:] for f in four], axis=0)
        q_ref[r] = (dot(own, qkg_ref[:, :CH], NN) * (HD ** (-0.5) * LOG2E)).astype(BF)
        gate_ref[r] = jax.nn.sigmoid(dot(own, qkg_ref[:, 3 * CH :], NN))
        kv_ref[r] = dot(keys_in, qkg_ref[:, CH : 3 * CH], NN).astype(BF)


def project(own, prev, nxt, far, qkg):
    row = pl.BlockSpec((PR_ROWS, COLS, CH), lambda i: (i, 0, 0))
    return pl.pallas_call(
        project_kernel,
        grid=(ROWS // PR_ROWS,),
        out_shape=(
            jax.ShapeDtypeStruct((ROWS, COLS, CH), BF),
            jax.ShapeDtypeStruct((ROWS, COLS, CH), F32),
            jax.ShapeDtypeStruct((ROWS, 4 * COLS, 2 * CH), BF),
        ),
        in_specs=[row] * 4 + [VMEM],
        out_specs=[row, row, pl.BlockSpec((PR_ROWS, 4 * COLS, 2 * CH), lambda i: (i, 0, 0))],
        compiler_params=PARAMS,
        cost_estimate=pl.CostEstimate(flops=10**10, bytes_accessed=2 * 10**7, transcendentals=10**5),
        name="project",
    )(own, prev, nxt, far, qkg)


def attend_kernel(
    pos_ref, filt_ref, q_ref, gate_ref, kv_ref, pay0_ref, pay1_ref, wo_ref, out_ref, bias,
):
    i = pl.program_id(0)
    c, zh, x = pos_ref[2], pos_ref[3], pos_ref[4]

    @pl.when(i == 0)
    def _():
        first_lane = lax.broadcasted_iota(jnp.int32, (PAY, LANES), 1) < HALF

        def place(pair, carry):
            row0 = pl.multiple_of(pair * 2 * ROWS, 8)
            tails = []
            for rel, shift in enumerate((0, 3, 1, 2)):
                at = lax.rem(zh + 8 - x - shift, 4)
                p0 = pay0_ref[pair, at].astype(F32) * LOG2E
                p1 = pay1_ref[pair, at].astype(F32) * LOG2E
                heads = []
                for p in (jnp.where(c == 0, p0, p1), jnp.where(c == 0, p1, p0)):
                    m = COLS
                    heads.append(
                        p[:, :LANES] + jnp.where(first_lane, p[:, m : m + 1], p[:, m + 1 : m + 2])
                    )
                    tails.append(p[:, LANES:COLS] + p[:, m + 2 : m + 3])
                for h in range(HEADS):
                    cut = slice(h * ROWS, (h + 1) * ROWS)
                    bias[h, pl.ds(row0, 2 * ROWS), rel * LANES : (rel + 1) * LANES] = jnp.concatenate(
                        [heads[0][cut], heads[1][cut]], axis=0
                    )
            for half in range(2):
                t = tails[4 * half : 4 * half + 4]
                both = [jnp.concatenate([t[0], t[2]], axis=1), jnp.concatenate([t[1], t[3]], axis=1)]
                lane = (4 + half) * LANES
                for h in range(HEADS):
                    cut = slice(h * ROWS, (h + 1) * ROWS)
                    bias[h, pl.ds(row0, 2 * ROWS), lane : lane + LANES] = jnp.concatenate(
                        [both[0][cut], both[1][cut]], axis=0
                    )
            return carry

        lax.fori_loop(0, 8, place, 0, unroll=2)

    run = lax.broadcasted_iota(jnp.int32, (1, 4 * COLS), 1) // HALF
    lane_head = lax.broadcasted_iota(jnp.int32, (COLS, CH), 1) // HD
    for r in range(AT_ROWS):
        q, k = q_ref[r], kv_ref[r, :, :CH]
        v1 = jnp.concatenate([kv_ref[r, :, CH:], jnp.ones((4 * COLS, CH), BF)], axis=1)
        row_tile = (pos_ref[5] + i * AT_ROWS + r) // TILE
        pen = jnp.zeros((1, 4 * COLS), F32)
        for rel, shift in enumerate((0, 3, 1, 2)):
            col = lax.rem(x + shift, 4) * COLS
            for slot, start in ((2 * rel, 0), (2 * rel + 1, HALF), (8 + rel, LANES)):
                keep = filt_ref[row_tile, (col + start) // TILE]
                pen = jnp.where(run == slot, (keep.astype(F32) - 1.0) * 1000000000.0, pen)
        att = jnp.zeros((COLS, CH), F32)
        for h in range(HEADS):
            mine = lane_head == h
            qh = jnp.where(mine, q, jnp.zeros_like(q))
            s = dot(qh, k, NT) + bias[h] + pen
            p = jnp.exp2((s - jnp.max(s, axis=-1, keepdims=True)).astype(BF))
            o = dot(p, v1, NN)
            att = jnp.where(mine, o[:, :CH] / o[:, CH:], att)
        gated = (gate_ref[r] * att).astype(BF)
        out_ref[r] = dot(gated, wo_ref[...], NN).astype(BF)


def attend(pos, filt, q, gate, kv, pay0, pay1, wo):
    row = pl.BlockSpec((AT_ROWS, COLS, CH), lambda i: (i, 0, 0))
    keys = pl.BlockSpec((AT_ROWS, 4 * COLS, 2 * CH), lambda i: (i, 0, 0))
    return pl.pallas_call(
        attend_kernel,
        grid=(ROWS // AT_ROWS,),
        out_shape=jax.ShapeDtypeStruct((ROWS, COLS, CH), BF),
        in_specs=[SMEM, SMEM, row, row, keys] + [VMEM] * 3,
        out_specs=row,
        scratch_shapes=[pltpu.VMEM((HEADS, COLS, 4 * COLS), F32)],
        compiler_params=PARAMS,
        cost_estimate=pl.CostEstimate(flops=8 * 10**9, bytes_accessed=10**7, transcendentals=7 * 10**6),
        name="attend",
    )(pos, filt, q, gate, kv, pay0, pay1, wo)


ALL = ("zh", "zl", "y", "c", "x")
SWAP = [
    ((a * 16 + r) * 4 + b, (b * 16 + r) * 4 + a) for a in range(4) for r in range(16) for b in range(4)
]


SPREAD = [
    ((a * 16 + r) * 4 + (2 * a - b + 2) % 4, (b * 16 + r) * 4 + a)
    for a in range(4) for r in range(16) for b in range(4)
]


def gather_right(own):
    pp = lax.ppermute
    z = pp(own, "zl", ring(2, 1))
    up, down, far = [pp(own, "y", ring(4, k)) for k in (1, 3, 2)]
    zdown = pp(z, "y", ring(4, 3))
    zup, zfar = pp(up, "zl", ring(2, 1)), pp(far, "zl", ring(2, 1))
    mine = [own, z, up, down, far, zup, zdown, zfar]
    return mine + [pp(m, "c", ring(2, 1)) for m in mine]


def gather_bias_z(own):
    col = jnp.stack([own] + [lax.ppermute(own, "zh", ring(4, k)) for k in (1, 2, 3)])
    return jnp.broadcast_to(col[None], (8,) + col.shape)


def body(stack, emb, entry, final, qkg, offset, out_proj, filt):
    pp = lax.ppermute
    zh, zl = lax.axis_index("zh"), lax.axis_index("zl")
    y, c, x = lax.axis_index("y"), lax.axis_index("c"), lax.axis_index("x")
    left, right = msa_project(stack.transpose(1, 0, 2), entry.T)
    row0 = (zh * 16 + zl * 8 + y * 2 + c) * ROWS
    prepared = (
        final.reshape(PF, PF, CH).transpose(1, 0, 2),
        jnp.pad(offset.T, ((0, 4), (0, 0))),
        jnp.stack([zl, y, c, zh, x, row0]).astype(jnp.int32),
    )
    right, w, off, pos = lax.optimization_barrier((pp(right, ALL, SPREAD), *prepared))
    mid, norm, bias = opm(pos, left, gather_right(right), w, emb, off)

    prev, nxt = pp(norm, "x", ring(4, 1)), pp(norm, "x", ring(4, 3))
    bias, own = lax.optimization_barrier((pp(bias, ALL, SWAP), norm))
    far = pp(own, "x", ring(4, 2))
    col = gather_bias_z(bias)
    prev, nxt, far, col = lax.optimization_barrier((prev, nxt, far, col))
    q, gate, kv = project(norm, prev, nxt, far, qkg)
    pay0 = lax.all_to_all(col, ("zl", "y"), 0, 0, tiled=True)
    q, gate, kv, pay0 = lax.optimization_barrier((q, gate, kv, pay0))
    pay1 = pp(pay0, "c", ring(2, 1))
    update = attend(pos, filt, q, gate, kv, pay0, pay1, out_proj)
    return mid, update


def solution(mesh):
    fine = jax.sharding.Mesh(mesh.devices.reshape(4, 2, 4, 2, 4), ALL)
    dap = ("zh", "zl", "y", "c")
    in_specs = (P(None, dap, None), P(dap, "x", None), P(), P(), P(), P(), P(), P())
    out_specs = (P(dap, "x", None), P(dap, "x", None))
    return jax.shard_map(body, mesh=fine, in_specs=in_specs, out_specs=out_specs, check_vma=False)
```
